32 devices in a mesh: dp: 2 (over x), mp: 16 (over z, y, core).
Axes of the slice: x: 2, y: 2, z: 4, core: 2. Of those that a mesh axis runs over, the one named last changes fastest.
Arguments:
- tokens: bfloat16 [1024, 16384], P('dp', 'mp'), may hold values from -6 to 6
- block_weight: bfloat16 [7, 256, 32768], P(None, None, 'mp'), may hold values from -0.125 to 0.125
- left_factor: bfloat16 [16384, 256], P('mp'), may hold values from -0.046875 to 0.046875
- right_factor: bfloat16 [256, 32768], P(None, 'mp'), may hold values from -0.375 to 0.375
- out_cotangent: bfloat16 [1024, 32768], P('dp', 'mp'), may hold values from -6 to 6
Outputs:
- activated: bfloat16 [1024, 32768], P('dp', 'mp')
- input_grad: bfloat16 [1024, 16384], P('dp', 'mp')
- weight_grad: bfloat16 [7, 256, 32768], P(None, 'dp', 'mp')
- left_grad: bfloat16 [16384, 256], P('mp')
- right_grad: bfloat16 [256, 32768], P(None, 'mp')
The draws below stay inside these ranges and needn't reach their ends.
All inputs are finite; a program needn't handle non-finite values.
Results may differ from the reference program's by a relative error of at most 0.0062.
Values may be sent and summed in bfloat16 or wider, within the bound.
No kernel may reach another device: no remote copies, remote signals or barrier semaphores. Data moves between devices by JAX's collectives and lax.ppermute only.
A program may use at most 128 MiB of HBM per device.

```python
import jax
import jax.numpy as jnp
import numpy as np

D = 16384
FF = 32768
B = 256
K = 7
R = 256
TOKENS = 1024


def steps_of(own_key, dims, cuts, low, top_value):
    def one(dim, parts):
        draws = jax.random.uniform(jax.random.fold_in(jax.random.fold_in(own_key, 6), dim), (parts,), jnp.float32, low / len(cuts), top_value / len(cuts))
        return jnp.repeat(jnp.exp(draws), dims[dim] // parts).reshape((-1,) + (1,) * (len(dims) - dim - 1))

    loudness = one(*cuts[0])
    for cut in cuts[1:]:
        loudness = loudness * one(*cut)
    return loudness


def bell_draw(key, dims, scale, reach, shards=(), dtype=jnp.bfloat16):
    array = jax.random.normal(key, dims, jnp.float32) * scale
    if len(shards) > 0:
        array = steps_of(key, dims, shards, -0.22, 0.18) * array
    return jnp.clip(array, min=-reach, max=reach).astype(dtype)


def setup_inputs(seed: int = 0) -> dict:
    seeds = jax.random.split(jax.random.key(seed), 6)
    tokens = bell_draw(seeds[0], (TOKENS, D), 1.0, 6.0, ((0, 2), (1, 16)))
    block_weight = bell_draw(seeds[1], (K, B, FF), (K * B) ** -0.5, 0.125, ((2, 16),))
    left_factor = bell_draw(seeds[2], (D, R), D ** -0.5, 0.046875, ((0, 16),))
    right_factor = bell_draw(seeds[3], (R, FF), R ** -0.5, 0.375, ((1, 16),))
    out_cotangent = bell_draw(seeds[4], (TOKENS, FF), 1.0, 6.0, ((0, 2), (1, 16)))
    return dict(tokens=tokens, block_weight=block_weight, left_factor=left_factor, right_factor=right_factor, out_cotangent=out_cotangent)


gelu_scale = 0.7978845608028654
gelu_cubic = 0.044715


def gelu_parts(preact):
    inner = gelu_scale * (preact + gelu_cubic * preact * preact * preact)
    tangent = jnp.tanh(inner)
    value = 0.5 * preact * (1.0 + tangent)
    slope = 0.5 * (1.0 + tangent) + 0.5 * preact * (1.0 - tangent * tangent) * gelu_scale * (1.0 + 3.0 * gelu_cubic * preact * preact)
    return value, slope


def reference(tokens, block_weight, left_factor, right_factor, out_cotangent):
    tok_count = tokens.shape[0]
    group_count = D // B
    group_ids = np.arange(group_count)
    tok_blocks = tokens.reshape(tok_count, group_count, B)
    weight_views = block_weight.reshape(K, B, group_count, 2 * B)
    butterfly = jnp.zeros((tok_count, group_count, 2 * B), jnp.float32)
    for tap_index in range(K):
        offset = 0 if tap_index == 0 else 1 << (tap_index - 1)
        chosen = tok_blocks[:, group_ids ^ offset].astype(jnp.float32)
        butterfly = butterfly + jnp.einsum("ngc,cgh->ngh", chosen, weight_views[tap_index].astype(jnp.float32))
    latent = jnp.dot(tokens, left_factor, preferred_element_type=jnp.float32)
    latent_bf = latent.astype(jnp.bfloat16)
    preact = butterfly.reshape(tok_count, FF) + jnp.dot(latent_bf, right_factor, preferred_element_type=jnp.float32)
    value, slope = gelu_parts(preact)
    activated = value.astype(jnp.bfloat16)
    grad_pre = (out_cotangent.astype(jnp.float32) * slope).astype(jnp.bfloat16)
    latent_grad = jnp.dot(grad_pre, right_factor.T, preferred_element_type=jnp.float32).astype(jnp.bfloat16)
    left_grad = jnp.dot(tokens.T, latent_grad, preferred_element_type=jnp.float32).astype(jnp.bfloat16)
    right_grad = jnp.dot(latent_bf.T, grad_pre, preferred_element_type=jnp.float32).astype(jnp.bfloat16)
    grad_view = grad_pre.reshape(tok_count, group_count, 2 * B).astype(jnp.float32)
    input_grad = jnp.dot(latent_grad, left_factor.T, preferred_element_type=jnp.float32).reshape(tok_count, group_count, B)
    weight_parts = []
    for tap_index in range(K):
        offset = 0 if tap_index == 0 else 1 << (tap_index - 1)
        chosen = tok_blocks[:, group_ids ^ offset].astype(jnp.float32)
        weight_tap = weight_views[tap_index].astype(jnp.float32)
        contrib = jnp.einsum("ngh,cgh->ngc", grad_view, weight_tap)
        input_grad = input_grad + contrib[:, group_ids ^ offset]
        weight_parts.append(jnp.einsum("ngc,ngh->cgh", chosen, grad_view).reshape(B, FF))
    weight_grad = jnp.stack(weight_parts).astype(jnp.bfloat16)
    input_grad = input_grad.reshape(tok_count, D).astype(jnp.bfloat16)
    return activated, input_grad, weight_grad, left_grad, right_grad
```

```python
import functools

import jax
import jax.numpy as jnp
from jax import lax
from jax.experimental import pallas as pl
from jax.experimental.pallas import tpu as pltpu
from jax.sharding import PartitionSpec as P

gelu_scale = 0.7978845608028654
gelu_cubic = 0.044715
f32 = jnp.float32
bf16 = jnp.bfloat16
NT = (((1,), (1,)), ((), ()))
TN = (((0,), (0,)), ((), ()))
VMEM_BYTES = 48 * 1024 * 1024


def from_partner(shard, axis, distance):
    return lax.ppermute(shard, axis, [(i, i ^ 1 << distance) for i in range(lax.axis_size(axis))])


def gelu_parts(preact):
    inner = gelu_scale * (preact + gelu_cubic * preact * preact * preact)
    tangent = jnp.tanh(inner)
    value = 0.5 * preact * (1.0 + tangent)
    slope = 0.5 * (1.0 + tangent) + 0.5 * preact * (1.0 - tangent * tangent) * gelu_scale * (
        1.0 + 3.0 * gelu_cubic * preact * preact
    )
    return (value, slope)


def params():
    return pltpu.CompilerParams(vmem_limit_bytes=VMEM_BYTES)


def cost(flops, moved, transcendentals=0):
    return pl.CostEstimate(flops=flops, bytes_accessed=moved, transcendentals=transcendentals)


def forward_body(local_taps, remote_taps, aliased, idx_ref, *refs):
    refs = list(refs)
    take = lambda n: [refs.pop(0) for _ in range(n)]
    own = take(local_taps)
    remote = take(remote_taps)
    latent_refs = take(2)
    weight_ref, right_ref, cot_ref = take(3)
    take(1 if aliased else 0)
    act_ref, grad_ref = take(2)
    terms = take(remote_taps)
    local_ref, latent_term_ref = take(2)
    group = pl.program_id(0)
    taps, block, hidden = weight_ref.shape
    weights = weight_ref[...].reshape(taps * block, hidden)
    inputs = jnp.concatenate([r[...] for r in own + remote], axis=1)
    latent = jnp.concatenate([r[0] for r in latent_refs], axis=0)
    right = right_ref[...]
    preact = jnp.dot(inputs, weights, preferred_element_type=f32)
    preact = preact + jnp.dot(latent, right, preferred_element_type=f32)
    value, slope = gelu_parts(preact)
    act_ref[...] = value.astype(bf16)
    grad = (cot_ref[...].astype(f32) * slope).astype(bf16)
    grad_ref[...] = grad
    spread = lax.dot_general(grad, weights, NT, preferred_element_type=f32)
    for k in range(remote_taps):
        lo = (local_taps + k) * block
        terms[k][...] = spread[:, lo : lo + block].astype(bf16)

    @pl.when(group == 0)
    def _():
        local_ref[...] = jnp.zeros_like(local_ref)
        latent_term_ref[...] = jnp.zeros_like(latent_term_ref)

    for k in range(local_taps):
        target = group if k == 0 else group ^ (1 << (k - 1))
        cols = pl.ds(pl.multiple_of(target * block, block), block)
        local_ref[:, cols] += spread[:, k * block : (k + 1) * block]
    latent_term_ref[...] += lax.dot_general(grad, right, NT, preferred_element_type=f32)


def forward_chunk(chunk, idx, tokens, remote, latent, weight, right, cotangent, act_before):
    rows, width = remote[0].shape
    taps, block, hidden_local = weight.shape
    groups = width // block
    hidden = hidden_local // groups
    local_taps = taps - len(remote)
    quarter, rank = latent.shape[1:]
    own_spec = lambda k: pl.BlockSpec(
        (rows, block), lambda g, idx: (chunk, g if k == 0 else g ^ (1 << (k - 1)))
    )
    latent_spec = lambda k: pl.BlockSpec((1, quarter, rank), lambda g, idx: (idx[0] ^ k, 0, 0))
    in_specs = [own_spec(k) for k in range(local_taps)]
    in_specs += [pl.BlockSpec((rows, block), lambda g, idx: (0, g))] * len(remote)
    in_specs += [latent_spec(2 * chunk), latent_spec(2 * chunk + 1)]
    in_specs += [
        pl.BlockSpec((taps, block, hidden), lambda g, idx: (0, 0, g)),
        pl.BlockSpec((rank, hidden), lambda g, idx: (0, g)),
        pl.BlockSpec((rows, hidden), lambda g, idx: (chunk, g)),
    ]
    args = [tokens] * local_taps + list(remote) + [latent, latent, weight, right, cotangent]
    aliases = {}
    if act_before is not None:
        in_specs.append(pl.BlockSpec(memory_space=pl.ANY))
        args.append(act_before)
        aliases = {len(args): 0}
    out_specs = [
        pl.BlockSpec((rows, hidden), lambda g, idx: (chunk, g)),
        pl.BlockSpec((rows, hidden), lambda g, idx: (0, g)),
    ]
    out_specs += [pl.BlockSpec((rows, block), lambda g, idx: (0, g))] * len(remote)
    out_specs += [
        pl.BlockSpec((rows, width), lambda g, idx: (0, 0)),
        pl.BlockSpec((rows, rank), lambda g, idx: (0, 0)),
    ]
    shape = jax.ShapeDtypeStruct
    out_shape = [shape(cotangent.shape, bf16), shape((rows, hidden_local), bf16)]
    out_shape += [shape((rows, width), bf16)] * len(remote)
    out_shape += [shape((rows, width), f32), shape((rows, rank), f32)]
    outs = pl.pallas_call(
        functools.partial(forward_body, local_taps, len(remote), act_before is not None),
        grid_spec=pltpu.PrefetchScalarGridSpec(
            num_scalar_prefetch=1, grid=(groups,), in_specs=in_specs, out_specs=out_specs
        ),
        out_shape=out_shape,
        input_output_aliases=aliases,
        compiler_params=params(),
        cost_estimate=cost(
            4 * rows * hidden_local * (taps * block + rank),
            2 * (weight.size + right.size + 3 * rows * hidden_local + 12 * rows * width),
            rows * hidden_local,
        ),
        name="forward_chunk",
    )(idx, *args)
    act, grad = outs[:2]
    return act, grad, outs[2 : 2 + len(remote)], outs[-2], outs[-1]


def halves_body(idx_ref, *refs):
    for src, dst in zip(refs[: len(refs) // 2], refs[len(refs) // 2 :]):
        dst[...] = src[...]


def column_halves(which, arrays, block):
    rows, width = arrays[0].shape
    half = block // 2
    return pl.pallas_call(
        halves_body,
        grid_spec=pltpu.PrefetchScalarGridSpec(
            num_scalar_prefetch=1,
            grid=(width // block,),
            in_specs=[pl.BlockSpec((rows, half), lambda j, which: (0, 2 * j + which[0]))]
            * len(arrays),
            out_specs=[pl.BlockSpec((rows, half), lambda j, which: (0, j))] * len(arrays),
        ),
        out_shape=[jax.ShapeDtypeStruct((rows, width // 2), bf16)] * len(arrays),
        compiler_params=params(),
        cost_estimate=cost(0, 2 * rows * width * len(arrays)),
        name="column_halves",
    )(which, *arrays)


def in_dp_order(idx_ref, near, far):
    first = idx_ref[1] == 0
    return jnp.concatenate([jnp.where(first, near, far), jnp.where(first, far, near)], axis=0)


def weights_body(local_taps, remote_taps, idx_ref, *refs):
    refs = list(refs)
    take = lambda n: [refs.pop(0)[...] for _ in range(n)]
    own = take(local_taps)
    remote = [jnp.concatenate(take(2), axis=0) for _ in range(remote_taps)]
    far_own = take(local_taps)
    far_remote = [jnp.concatenate(take(2), axis=0) for _ in range(remote_taps)]
    grad = jnp.concatenate(take(2), axis=0)
    far_grad = jnp.concatenate(take(2), axis=0)
    latent_ref, far_latent_ref, weight_ref, right_ref = refs
    order = [k ^ idx_ref[0] for k in range(latent_ref.shape[0])]
    latent = jnp.concatenate([latent_ref[k] for k in order], axis=0)
    far_latent = jnp.concatenate([far_latent_ref[k] for k in order], axis=0)
    near = jnp.concatenate(own + remote, axis=1)
    far = jnp.concatenate(far_own + far_remote, axis=1)
    total = lax.dot_general(near, grad, TN, preferred_element_type=f32)
    total = total + lax.dot_general(far, far_grad, TN, preferred_element_type=f32)
    weight_ref[...] = total.reshape(weight_ref.shape).astype(bf16)
    latents, grads = in_dp_order(idx_ref, latent, far_latent), in_dp_order(idx_ref, grad, far_grad)
    right = lax.dot_general(latents, grads, TN, preferred_element_type=f32)
    right_ref[...] = right.astype(bf16)


def weight_grads(idx, tokens, remote, far_tokens, far_remote, grads, latent, far_latent, taps, block):
    rows, width = tokens.shape
    chunk_rows = grads[0].shape[0]
    hidden_local = grads[0].shape[1]
    groups = width // block
    half = block // 2
    hidden = hidden_local // groups
    local_taps = taps - len(remote)
    rank = latent.shape[2]
    own_spec = lambda k: pl.BlockSpec(
        (rows, half), lambda g, idx: (0, 2 * (g if k == 0 else g ^ (1 << (k - 1))) + idx[1])
    )
    own_specs = [own_spec(k) for k in range(local_taps)]
    remote_specs = [pl.BlockSpec((chunk_rows, half), lambda g, idx: (0, 2 * g + idx[1]))] * (
        2 * len(remote)
    )
    far_specs = [pl.BlockSpec((chunk_rows, half), lambda g, idx: (0, g))] * (2 * len(remote))
    grad_specs = [pl.BlockSpec((chunk_rows, hidden), lambda g, idx: (0, g))] * 4
    latent_spec = pl.BlockSpec(latent.shape, lambda g, idx: (0, 0, 0))
    return pl.pallas_call(
        functools.partial(weights_body, local_taps, len(remote)),
        grid_spec=pltpu.PrefetchScalarGridSpec(
            num_scalar_prefetch=1,
            grid=(groups,),
            in_specs=own_specs + remote_specs + own_specs + far_specs + grad_specs + [latent_spec] * 2,
            out_specs=[
                pl.BlockSpec((taps, half, hidden), lambda g, idx: (0, 0, g)),
                pl.BlockSpec((rank, hidden), lambda g, idx: (0, g)),
            ],
        ),
        out_shape=[
            jax.ShapeDtypeStruct((taps, half, hidden_local), bf16),
            jax.ShapeDtypeStruct((rank, hidden_local), bf16),
        ],
        compiler_params=params(),
        cost_estimate=cost(
            4 * rows * hidden_local * (taps * half + rank),
            2 * (taps * half * hidden_local + 4 * rows * hidden_local + 10 * rows * width),
        ),
        name="weight_grads",
    )(
        idx,
        *([tokens] * local_taps),
        *[c for pair in remote for c in pair],
        *([far_tokens] * local_taps),
        *[c for pair in far_remote for c in pair],
        *grads,
        latent,
        far_latent,
    )


def inputs_body(n_terms, idx_ref, *refs):
    refs = list(refs)
    pair = lambda: jnp.concatenate([refs.pop(0)[...], refs.pop(0)[...]], axis=0)
    total = pair()
    for _ in range(n_terms):
        total = total + pair().astype(f32)
    tokens_ref, far_tokens_ref, left_ref, latent_ref, far_latent_ref, input_ref, left_grad_ref = refs
    order = [k ^ idx_ref[0] for k in range(latent_ref.shape[0])]
    latent = jnp.concatenate([latent_ref[k] for k in order], axis=0)
    far_latent = jnp.concatenate([far_latent_ref[k] for k in order], axis=0)
    low_rank = lax.dot_general(latent, left_ref[...], NT, preferred_element_type=f32)
    input_ref[...] = (total + low_rank).astype(bf16)
    tokens = in_dp_order(idx_ref, tokens_ref[...], far_tokens_ref[...])
    latents = in_dp_order(idx_ref, latent, far_latent)
    left = lax.dot_general(tokens, latents, TN, preferred_element_type=f32)
    left_grad_ref[...] = left.astype(bf16)


def input_grads(idx, local, terms, tokens, far_tokens, left, latent, far_latent, block):
    rows, width = tokens.shape
    rank = left.shape[1]
    chunk_rows = local[0].shape[0]
    chunk_spec = pl.BlockSpec((chunk_rows, block), lambda g, idx: (0, g))
    token_spec = pl.BlockSpec((rows, block), lambda g, idx: (0, g))
    left_spec = pl.BlockSpec((block, rank), lambda g, idx: (g, 0))
    latent_spec = pl.BlockSpec(latent.shape, lambda g, idx: (0, 0, 0))
    return pl.pallas_call(
        functools.partial(inputs_body, len(terms)),
        grid_spec=pltpu.PrefetchScalarGridSpec(
            num_scalar_prefetch=1,
            grid=(width // block,),
            in_specs=[chunk_spec] * (2 + 2 * len(terms))
            + [token_spec, token_spec, left_spec, latent_spec, latent_spec],
            out_specs=[token_spec, left_spec],
        ),
        out_shape=[
            jax.ShapeDtypeStruct(tokens.shape, bf16),
            jax.ShapeDtypeStruct(left.shape, bf16),
        ],
        compiler_params=params(),
        cost_estimate=cost(6 * rows * width * rank, 20 * rows * width),
        name="input_grads",
    )(idx, *local, *[c for pair in terms for c in pair], tokens, far_tokens, left, latent, far_latent)


def summed_over_mp(part):
    bits = lax.axis_size("mp").bit_length() - 1
    index = lax.axis_index("mp")
    for bit in range(2):
        half = part.shape[0] // 2
        mine = (index >> bit) & 1
        sent = lax.dynamic_slice_in_dim(part, (1 - mine) * half, half, 0)
        kept = lax.dynamic_slice_in_dim(part, mine * half, half, 0)
        part = kept + from_partner(sent, "mp", bit)
    for bit in range(2, bits):
        part = part + from_partner(part, "mp", bit)
    stack = part.astype(bf16)[None]
    for bit in (1, 0):
        stack = jnp.concatenate([stack, from_partner(stack, "mp", bit)], axis=0)
    return stack


def on_device(tokens, block_weight, left_factor, right_factor, out_cotangent):
    rows, width = tokens.shape
    taps, block, _ = block_weight.shape
    groups = width // block
    local_bits = groups.bit_length() - 1
    remote_bits = range(taps - 1 - local_bits)
    mp_index = lax.axis_index("mp")
    dp_index = lax.axis_index("dp")
    place = 2 * (mp_index & 1) + ((mp_index >> 1) & 1)
    idx = jnp.stack([place, dp_index]).astype(jnp.int32)
    mine = dp_index.reshape(1).astype(jnp.int32)
    theirs = 1 - mine
    half_rows = rows // 2
    chunks = [tokens[:half_rows], tokens[half_rows:]]

    received = [[from_partner(c, "mp", bit) for bit in remote_bits] for c in chunks]
    far_tokens = from_partner(tokens, "dp", 0)
    latent = summed_over_mp(jnp.dot(tokens, left_factor, preferred_element_type=f32))
    far_latent = from_partner(latent, "dp", 0)

    act, grads, far_grads, terms, local, latent_terms = None, [], [], [], [], []
    far_received = []
    for chunk in range(2):
        sent = column_halves(theirs, received[chunk][2:], block)
        far_received.append([from_partner(c, "dp", 0) for c in sent])
        act, grad, out_terms, local_sum, latent_term = forward_chunk(
            chunk, idx, tokens, received[chunk], latent, block_weight, right_factor, out_cotangent, act
        )
        terms.append([from_partner(t, "mp", bit) for bit, t in zip(remote_bits, out_terms)])
        far_grads.append(from_partner(grad, "dp", 0))
        grads.append(grad)
        local.append(local_sum)
        latent_terms.append(latent_term)
    far_half = column_halves(mine, [far_tokens], block)[0]
    far_low = [from_partner(far_half, "mp", bit) for bit in remote_bits[:2]]
    far_low = [[c[:half_rows], c[half_rows:]] for c in far_low]
    far_pairs = far_low + [list(p) for p in zip(*far_received)]

    latent_grad = summed_over_mp(jnp.concatenate(latent_terms, axis=0))
    far_latent_grad = from_partner(latent_grad, "dp", 0)
    weight_grad, right_grad = weight_grads(
        idx,
        tokens,
        list(zip(*received)),
        far_tokens,
        far_pairs,
        grads + far_grads,
        latent,
        far_latent,
        taps,
        block,
    )
    input_grad, left_grad = input_grads(
        idx,
        local,
        list(zip(*terms)),
        tokens,
        far_tokens,
        left_factor,
        latent_grad,
        far_latent_grad,
        block,
    )
    return act, input_grad, weight_grad, left_grad, right_grad


def flip_groups(blocks, distance):
    full_shape = blocks.shape
    group_count = full_shape[1]
    split_view = blocks.reshape(
        (full_shape[0], group_count // (2 * distance), 2, distance) + full_shape[2:]
    )
    return jnp.flip(split_view, axis=2).reshape(full_shape)


def on_device_general(tokens, block_weight, left_factor, right_factor, out_cotangent):
    tok_rows = tokens.shape[0]
    local_width = tokens.shape[1]
    tap_count = block_weight.shape[0]
    block_size = block_weight.shape[1]
    hidden_local = block_weight.shape[2]
    group_count = local_width // block_size
    local_bits = group_count.bit_length() - 1
    tok_blocks = tokens.reshape(tok_rows, group_count, block_size)
    tap_inputs = [tok_blocks]
    for tap_index in range(1, tap_count):
        level_bit = tap_index - 1
        if level_bit < local_bits:
            tap_inputs.append(flip_groups(tok_blocks, 1 << level_bit))
        else:
            partner = from_partner(tokens, "mp", level_bit - local_bits)
            tap_inputs.append(partner.reshape(tok_rows, group_count, block_size))
    stacked = jnp.stack(tap_inputs, axis=2)
    weight_view = block_weight.reshape(tap_count, block_size, group_count, 2 * block_size)
    butterfly = jnp.einsum("tgkc,kcgh->tgh", stacked, weight_view, preferred_element_type=f32)
    butterfly = butterfly.reshape(tok_rows, hidden_local)
    latent = lax.psum(jnp.dot(tokens, left_factor, preferred_element_type=f32), "mp")
    latent_bf = latent.astype(bf16)
    preact = butterfly + jnp.dot(latent_bf, right_factor, preferred_element_type=f32)
    value, slope = gelu_parts(preact)
    activated = value.astype(bf16)
    grad_pre = (out_cotangent.astype(f32) * slope).astype(bf16)
    latent_term = lax.dot_general(grad_pre, right_factor, NT, preferred_element_type=f32)
    latent_grad = lax.psum(latent_term, "mp").astype(bf16)
    left_part = lax.dot_general(tokens, latent_grad, TN, preferred_element_type=f32)
    right_part = lax.dot_general(latent_bf, grad_pre, TN, preferred_element_type=f32)
    left_sum, right_sum = lax.psum((left_part, right_part), "dp")
    grad_view = grad_pre.reshape(tok_rows, group_count, 2 * block_size)
    spread = jnp.einsum("tgh,kcgh->tgkc", grad_view, weight_view, preferred_element_type=f32)
    input_sum = spread[:, :, 0]
    for tap_index in range(1, tap_count):
        level_bit = tap_index - 1
        piece = spread[:, :, tap_index]
        if level_bit < local_bits:
            input_sum = input_sum + flip_groups(piece, 1 << level_bit)
        else:
            returned = from_partner(
                piece.reshape(tok_rows, local_width), "mp", level_bit - local_bits
            )
            input_sum = input_sum + returned.reshape(tok_rows, group_count, block_size)
    low_rank = lax.dot_general(latent_grad, left_factor, NT, preferred_element_type=f32)
    input_grad = (input_sum.reshape(tok_rows, local_width) + low_rank).astype(bf16)
    partial_value = jnp.einsum("tgkc,tgh->kcgh", stacked, grad_view, preferred_element_type=f32)
    partial_value = partial_value.reshape(tap_count, block_size, hidden_local)
    weight_grad = lax.psum_scatter(partial_value, "dp", scatter_dimension=1, tiled=True).astype(bf16)
    return (activated, input_grad, weight_grad, left_sum.astype(bf16), right_sum.astype(bf16))


def solution(mesh):
    pairs = mesh.shape["dp"] == 2 and mesh.shape["mp"] >= 4
    return jax.shard_map(
        on_device if pairs else on_device_general,
        mesh=mesh,
        in_specs=(P("dp", "mp"), P(None, None, "mp"), P("mp", None), P(None, "mp"), P("dp", "mp")),
        out_specs=(P("dp", "mp"), P("dp", "mp"), P(None, "dp", "mp"), P("mp", None), P(None, "mp")),
        check_vma=False,
    )
```

```python
import functools

import jax
import jax.numpy as jnp
from jax import lax
from jax.experimental import pallas as pl
from jax.experimental.pallas import tpu as pltpu
from jax.sharding import PartitionSpec as P

gelu_scale = 0.7978845608028654
gelu_cubic = 0.044715
f32 = jnp.float32
bf16 = jnp.bfloat16
NEAR_HINT = 8
FORWARD_HINTS = (4, 1 / 16)
WEIGHT_HINT = 1 / 16
INPUT_HINT = 30
LEFT_HINT = 1 / 16
NT = (((1,), (1,)), ((), ()))
TN = (((0,), (0,)), ((), ()))


def from_partner(shard, axis, distance):
    return lax.ppermute(shard, axis, [(i, i ^ 1 << distance) for i in range(lax.axis_size(axis))])


def gelu_parts(preact):
    inner = gelu_scale * (preact + gelu_cubic * preact * preact * preact)
    tangent = jnp.tanh(inner)
    value = 0.5 * preact * (1.0 + tangent)
    slope = 0.5 * (1.0 + tangent) + 0.5 * preact * (1.0 - tangent * tangent) * gelu_scale * (
        1.0 + 3.0 * gelu_cubic * preact * preact
    )
    return (value, slope)


def params(mib=60):
    return pltpu.CompilerParams(vmem_limit_bytes=mib * 1024 * 1024)


def cost(hint, flops, moved):
    return pl.CostEstimate(flops=int(hint * flops), bytes_accessed=int(hint * moved), transcendentals=0)


def rows_of(pieces):
    return pieces[0][...] if len(pieces) == 1 else jnp.concatenate([p[...] for p in pieces], axis=0)


def taken(refs):
    refs = list(refs)
    return lambda n: [refs.pop(0) for _ in range(n)]


def forward_body(local_taps, pieces, aliased, packed, idx_ref, *refs):
    take = taken(refs)
    own = [r[...] for r in take(local_taps)]
    remote_refs = [take(n) for n in pieces]
    remote = [rows_of(r) for r in remote_refs]
    remote_refs = [r[0] for r in remote_refs]
    latent = jnp.concatenate([r[0] for r in take(2)], axis=0)
    weight_ref, right_ref, cot_ref = take(3)
    take(1 if aliased else 0)
    act_ref, grad_ref = take(2)
    terms = take(len(pieces))
    local_ref, latent_term_ref = take(2)
    group = pl.program_id(0)
    taps, block, hidden = weight_ref.shape
    weights = weight_ref[...].reshape(taps * block, hidden)
    right = right_ref[...]
    preact = jnp.dot(jnp.concatenate(own + remote, axis=1), weights, preferred_element_type=f32)
    preact = preact + jnp.dot(latent, right, preferred_element_type=f32)
    value, slope = gelu_parts(preact)
    act_ref[...] = value.astype(bf16)
    grad = (cot_ref[...].astype(f32) * slope).astype(bf16)
    rows = grad.shape[0]
    grad_ref[:rows] = grad
    if packed:
        half = block // 2
        height = grad_ref.shape[0] - rows
        theirs = pl.ds(pl.multiple_of((1 - idx_ref[1]) * half, half), half)
        cells = [
            ref[row : row + height, theirs] for ref in remote_refs[-packed:] for row in range(0, rows, height)
        ]
        grad_ref[rows:] = jnp.concatenate(cells, axis=1)
    spread = lax.dot_general(grad, weights, NT, preferred_element_type=f32)
    for k, term_ref in enumerate(terms):
        lo = (local_taps + k) * block
        term_ref[...] = spread[:, lo : lo + block].astype(bf16)

    @pl.when(group == 0)
    def _():
        local_ref[...] = jnp.zeros_like(local_ref)
        latent_term_ref[...] = jnp.zeros_like(latent_term_ref)

    for k in range(local_taps):
        target = group if k == 0 else group ^ (1 << (k - 1))
        cols = pl.ds(pl.multiple_of(target * block, block), block)
        local_ref[:, cols] += spread[:, k * block : (k + 1) * block]
    latent_term_ref[...] += lax.dot_general(grad, right, NT, preferred_element_type=f32)


def forward_chunk(chunk, idx, tokens, remote, latent, weight, right, cotangent, act_before, packed):
    taps, block, hidden_local = weight.shape
    width = tokens.shape[1]
    rows = tokens.shape[0] // 2
    groups = width // block
    hidden = hidden_local // groups
    local_taps = taps - len(remote)
    quarter, rank = latent.shape[2:]
    height = packed * rows * (block // 2) // hidden
    own_spec = lambda k: pl.BlockSpec(
        (rows, block), lambda g, idx: (chunk, g if k == 0 else g ^ (1 << (k - 1)))
    )
    piece_spec = lambda piece: pl.BlockSpec((piece[2], block), lambda g, idx: (piece[1], g))
    latent_spec = lambda k: pl.BlockSpec(
        (1, None, quarter, rank), lambda g, idx: (idx[0] ^ k, 0, 0, 0)
    )
    in_specs = [own_spec(k) for k in range(local_taps)]
    in_specs += [piece_spec(p) for tap in remote for p in tap]
    in_specs += [latent_spec(2 * chunk), latent_spec(2 * chunk + 1)]
    in_specs += [
        pl.BlockSpec((taps, block, hidden), lambda g, idx: (0, 0, g)),
        pl.BlockSpec((rank, hidden), lambda g, idx: (0, g)),
        pl.BlockSpec((rows, hidden), lambda g, idx: (chunk, g)),
    ]
    args = [tokens] * local_taps + [p[0] for tap in remote for p in tap]
    args += [latent, latent, weight, right, cotangent]
    aliases = {}
    if act_before is not None:
        in_specs.append(pl.BlockSpec(memory_space=pl.ANY))
        args.append(act_before)
        aliases = {len(args): 0}
    out_specs = [
        pl.BlockSpec((rows, hidden), lambda g, idx: (chunk, g)),
        pl.BlockSpec((rows + height, hidden), lambda g, idx: (0, g)),
    ]
    out_specs += [pl.BlockSpec((rows, block), lambda g, idx: (0, g))] * len(remote)
    out_specs += [
        pl.BlockSpec((rows, width), lambda g, idx: (0, 0)),
        pl.BlockSpec((rows, rank), lambda g, idx: (0, 0)),
    ]
    shape = jax.ShapeDtypeStruct
    out_shape = [shape(cotangent.shape, bf16), shape((rows + height, hidden_local), bf16)]
    out_shape += [shape((rows, width), bf16)] * len(remote)
    out_shape += [shape((rows, width), f32), shape((rows, rank), f32)]
    outs = pl.pallas_call(
        functools.partial(
            forward_body, local_taps, [len(t) for t in remote], act_before is not None, packed
        ),
        grid_spec=pltpu.PrefetchScalarGridSpec(
            num_scalar_prefetch=1, grid=(groups,), in_specs=in_specs, out_specs=out_specs
        ),
        out_shape=out_shape,
        input_output_aliases=aliases,
        compiler_params=params(),
        cost_estimate=cost(
            FORWARD_HINTS[chunk],
            4 * rows * hidden_local * (taps * block + rank),
            2 * (weight.size + right.size + 3 * rows * hidden_local + 12 * rows * width),
        ),
        name="forward_chunk",
    )(idx, *args)
    act, grad = outs[:2]
    return act, grad, outs[2 : 2 + len(remote)], outs[-2], outs[-1]


def halves_body(idx_ref, *refs):
    row, out_ref = 0, refs[-1]
    for src in refs[:-1]:
        out_ref[row : row + src.shape[0]] = src[...]
        row += src.shape[0]


def column_halves(which, arrays, block):
    width = arrays[0].shape[1]
    half = block // 2
    rows = sum(a.shape[0] for a in arrays)
    return pl.pallas_call(
        halves_body,
        grid_spec=pltpu.PrefetchScalarGridSpec(
            num_scalar_prefetch=1,
            grid=(width // block,),
            in_specs=[
                pl.BlockSpec((a.shape[0], half), lambda j, which: (0, 2 * j + which[0])) for a in arrays
            ],
            out_specs=pl.BlockSpec((rows, half), lambda j, which: (0, j)),
        ),
        out_shape=jax.ShapeDtypeStruct((rows, width // 2), bf16),
        compiler_params=params(8),
        cost_estimate=cost(1 / 16, 0, 2 * rows * width),
        name="column_halves",
    )(which, *arrays)


def in_dp_order(idx_ref, near, far):
    first = idx_ref[1] == 0
    return jnp.concatenate([jnp.where(first, near, far), jnp.where(first, far, near)], axis=0)


def near_body(local_taps, pieces, idx_ref, *refs):
    take = taken(refs)
    own = [r[...] for r in take(local_taps)]
    remote = [rows_of(take(n)) for n in pieces]
    grad = rows_of(take(2))
    sum_ref = refs[-1]
    total = lax.dot_general(jnp.concatenate(own + remote, axis=1), grad, TN, preferred_element_type=f32)
    sum_ref[...] = total.reshape(sum_ref.shape)


def far_body(local_taps, pieces, packed, idx_ref, *refs):
    take = taken(refs)
    own = [r[...] for r in take(local_taps)]
    remote = [rows_of(take(n)) for n in pieces]
    pack_ref = take(1)[0]
    half = own[0].shape[1]
    cells = [pack_ref[:, lo : lo + half] for lo in range(0, pack_ref.shape[1], half)]
    count = len(cells) // packed
    for k in range(packed):
        tap = len(remote) - packed + k
        remote[tap] = jnp.concatenate([remote[tap]] + cells[k * count : (k + 1) * count], axis=0)
    grad, far_grad = rows_of(take(2)), rows_of(take(2))
    latent_ref, far_latent_ref, near_ref, weight_ref, right_ref = take(5)
    total = lax.dot_general(jnp.concatenate(own + remote, axis=1), far_grad, TN, preferred_element_type=f32)
    weight_ref[...] = (near_ref[...] + total.reshape(weight_ref.shape)).astype(bf16)
    order = [k ^ idx_ref[0] for k in range(latent_ref.shape[0])]
    latent = jnp.concatenate([latent_ref[k] for k in order], axis=0)
    far_latent = jnp.concatenate([far_latent_ref[k] for k in order], axis=0)
    latents, grads = in_dp_order(idx_ref, latent, far_latent), in_dp_order(idx_ref, grad, far_grad)
    right = lax.dot_general(latents, grads, TN, preferred_element_type=f32)
    right_ref[...] = right.astype(bf16)


def weight_specs(tokens, grads, taps, block):
    rows, width = tokens.shape
    chunk_rows, hidden_local = grads[0].shape
    groups = width // block
    half = block // 2
    hidden = hidden_local // groups
    own_spec = lambda k: pl.BlockSpec(
        (rows, half), lambda g, idx: (0, 2 * (g if k == 0 else g ^ (1 << (k - 1))) + idx[1])
    )
    grad_spec = pl.BlockSpec((chunk_rows, hidden), lambda g, idx: (0, g))
    sum_spec = pl.BlockSpec((taps, half, hidden), lambda g, idx: (0, 0, g))
    return rows, chunk_rows, hidden_local, groups, half, hidden, own_spec, grad_spec, sum_spec


def near_weight_grads(idx, tokens, remote, grads, taps, block):
    rows, _, hidden_local, groups, half, _, own_spec, grad_spec, sum_spec = weight_specs(
        tokens, grads, taps, block
    )
    local_taps = taps - len(remote)
    piece_spec = lambda p: pl.BlockSpec((p[2], half), lambda g, idx: (p[1], 2 * g + idx[1]))
    pieces = [p for tap in remote for p in tap]
    return pl.pallas_call(
        functools.partial(near_body, local_taps, [len(t) for t in remote]),
        grid_spec=pltpu.PrefetchScalarGridSpec(
            num_scalar_prefetch=1,
            grid=(groups,),
            in_specs=[own_spec(k) for k in range(local_taps)]
            + [piece_spec(p) for p in pieces]
            + [grad_spec] * 2,
            out_specs=sum_spec,
        ),
        out_shape=jax.ShapeDtypeStruct((taps, half, hidden_local), f32),
        compiler_params=params(),
        cost_estimate=cost(
            NEAR_HINT, 2 * rows * hidden_local * taps * half, 4 * taps * half * hidden_local
        ),
        name="near_weight_grads",
    )(idx, *([tokens] * local_taps), *[p[0] for p in pieces], *grads)


def weight_grads(idx, near, tokens, remote, grads, latent, far_latent, taps, block):
    rows, chunk_rows, hidden_local, groups, half, hidden, own_spec, grad_spec, sum_spec = weight_specs(
        tokens, grads, taps, block
    )
    local_taps = taps - len(remote)
    rank = latent[0].shape[3]
    pack = grads[-1]
    height = pack.shape[0] - chunk_rows
    packed = height * hidden // (chunk_rows * half)
    piece_spec = lambda p: pl.BlockSpec((p[2], half), lambda g, idx: (p[1], g))
    pieces = [p for tap in remote for p in tap]
    return pl.pallas_call(
        functools.partial(far_body, local_taps, [len(t) for t in remote], packed),
        grid_spec=pltpu.PrefetchScalarGridSpec(
            num_scalar_prefetch=1,
            grid=(groups,),
            in_specs=[own_spec(k) for k in range(local_taps)]
            + [piece_spec(p) for p in pieces]
            + [pl.BlockSpec((height, hidden), lambda g, idx: (chunk_rows // height, g))]
            + [grad_spec] * 4
            + [latent_spec(latent), latent_spec(far_latent), sum_spec],
            out_specs=[sum_spec, pl.BlockSpec((rank, hidden), lambda g, idx: (0, g))],
        ),
        out_shape=[
            jax.ShapeDtypeStruct((taps, half, hidden_local), bf16),
            jax.ShapeDtypeStruct((rank, hidden_local), bf16),
        ],
        compiler_params=params(),
        cost_estimate=cost(
            WEIGHT_HINT,
            2 * rows * hidden_local * (taps * half + 2 * rank),
            8 * taps * half * hidden_local,
        ),
        name="weight_grads",
    )(
        idx,
        *([tokens] * local_taps),
        *[p[0] for p in pieces],
        pack,
        *grads,
        latent[0],
        far_latent[0],
        near,
    )


def inputs_body(n_terms, idx_ref, *refs):
    take = taken(refs)
    total = rows_of(take(2))
    for _ in range(n_terms):
        total = total + rows_of(take(2)).astype(f32)
    left_ref, latent_ref, input_ref = take(3)
    latent = jnp.concatenate([latent_ref[k ^ idx_ref[0]] for k in range(latent_ref.shape[0])], axis=0)
    low_rank = lax.dot_general(latent, left_ref[...], NT, preferred_element_type=f32)
    input_ref[...] = (total + low_rank).astype(bf16)


def latent_spec(pair):
    return pl.BlockSpec(
        (pair[0].shape[0], None) + pair[0].shape[2:], lambda g, idx: (0, pair[1], 0, 0)
    )


def input_grads(idx, local, terms, left, latent, block):
    width, rank = left.shape
    chunk_rows = local[0].shape[0]
    rows = 2 * chunk_rows
    chunk_spec = pl.BlockSpec((chunk_rows, block), lambda g, idx: (0, g))
    return pl.pallas_call(
        functools.partial(inputs_body, len(terms)),
        grid_spec=pltpu.PrefetchScalarGridSpec(
            num_scalar_prefetch=1,
            grid=(width // block,),
            in_specs=[chunk_spec] * (2 + 2 * len(terms))
            + [pl.BlockSpec((block, rank), lambda g, idx: (g, 0)), latent_spec(latent)],
            out_specs=pl.BlockSpec((rows, block), lambda g, idx: (0, g)),
        ),
        out_shape=jax.ShapeDtypeStruct((rows, width), bf16),
        compiler_params=params(),
        cost_estimate=cost(INPUT_HINT, 2 * rows * width * rank, 20 * rows * width),
        name="input_grads",
    )(idx, *local, *[c for pair in terms for c in pair], left, latent[0])


def left_body(idx_ref, tokens_ref, far_tokens_ref, latent_ref, far_latent_ref, left_ref):
    order = [k ^ idx_ref[0] for k in range(latent_ref.shape[0])]
    latent = jnp.concatenate([latent_ref[k] for k in order], axis=0)
    far_latent = jnp.concatenate([far_latent_ref[k] for k in order], axis=0)
    tokens = in_dp_order(idx_ref, tokens_ref[...], far_tokens_ref[...])
    latents = in_dp_order(idx_ref, latent, far_latent)
    left = lax.dot_general(tokens, latents, TN, preferred_element_type=f32)
    left_ref[...] = left.astype(bf16)


def left_grads(idx, tokens, far_tokens, latent, far_latent, block):
    rows, width = tokens.shape
    rank = latent[0].shape[3]
    token_spec = pl.BlockSpec((rows, block), lambda g, idx: (0, g))
    return pl.pallas_call(
        left_body,
        grid_spec=pltpu.PrefetchScalarGridSpec(
            num_scalar_prefetch=1,
            grid=(width // block,),
            in_specs=[token_spec, token_spec, latent_spec(latent), latent_spec(far_latent)],
            out_specs=pl.BlockSpec((block, rank), lambda g, idx: (g, 0)),
        ),
        out_shape=jax.ShapeDtypeStruct((width, rank), bf16),
        compiler_params=params(),
        cost_estimate=cost(LEFT_HINT, 4 * rows * width * rank, 4 * rows * width),
        name="left_grads",
    )(idx, tokens, far_tokens, latent[0], far_latent[0])


def after(value, *first):
    return lax.optimization_barrier((value, first))[0]


def one_step(f, *args):
    shapes = jax.eval_shape(f, *args)
    other = lambda *_: jax.tree.map(lambda x: jnp.zeros(x.shape, x.dtype), shapes)
    return lax.cond(lax.axis_index("mp") >= 0, f, other, *args)


def halved_sum(halves, bit):
    mine = (lax.axis_index("mp") >> bit) & 1
    sent = jnp.where(mine == 0, halves[1], halves[0])
    kept = jnp.where(mine == 0, halves[0], halves[1])
    return kept + from_partner(sent, "mp", bit)


def high_sum(part):
    for bit in range(2, lax.axis_size("mp").bit_length() - 1):
        part = part + from_partner(part, "mp", bit)
    return part.astype(bf16)[None, None]


def gathered(stack):
    for bit in (1, 0):
        stack = jnp.concatenate([stack, from_partner(stack, "mp", bit)], axis=0)
    return stack


def with_places(arrays, places):
    return [[(a, *p) for a, p in zip(*tap)] for tap in zip(arrays, places)]


def over_high_terms(terms, *first):
    return [from_partner(after(t, *first), "mp", bit) for bit, t in enumerate(terms) if bit >= 2]


def on_device(tokens, block_weight, left_factor, right_factor, out_cotangent):
    rows, width = tokens.shape
    taps, block, _ = block_weight.shape
    groups = width // block
    local_bits = groups.bit_length() - 1
    high_bits = range(2, taps - 1 - local_bits)
    mp_index = lax.axis_index("mp")
    dp_index = lax.axis_index("dp")
    place = 2 * (mp_index & 1) + ((mp_index >> 1) & 1)
    idx = jnp.stack([place, dp_index]).astype(jnp.int32)
    mine = dp_index.reshape(1).astype(jnp.int32)
    theirs = 1 - mine
    half_rows = rows // 2

    over_high = lambda x: [from_partner(x, "mp", bit) for bit in high_bits]
    cut = half_rows // 2
    first = over_high(tokens[:cut])

    def low_part(tokens, left):
        part = jnp.dot(tokens, left, preferred_element_type=f32)
        part = halved_sum(jnp.split(part, 2, axis=0), 0)
        core = from_partner(after(tokens, part), "mp", 0)
        return halved_sum(jnp.split(part, 2, axis=0), 1), core

    def high_part(part, tokens):
        far_tokens = from_partner(tokens, "dp", 0)
        near_y = from_partner(tokens[:half_rows], "mp", 1)
        quarter_sum = high_sum(part)
        second = over_high(after(tokens[cut:half_rows], quarter_sum))
        far = from_partner(quarter_sum, "dp", 0)
        far_half = column_halves(mine, [far_tokens], block)
        return gathered(quarter_sum), far, far_tokens, far_half, near_y, second

    low_sum, core = one_step(low_part, tokens, left_factor)
    low_sum, first = after((low_sum, first))
    latent, far_quarter, far_tokens, far_half, near_y, second = one_step(high_part, low_sum, tokens)
    third = over_high(after(tokens[half_rows:], latent))
    far_y = from_partner(after(tokens[half_rows:], latent), "mp", 1)
    received = [
        [[(core, 0, half_rows)], [(near_y, 0, half_rows)]]
        + [[(p, 0, cut), (q, 0, half_rows - cut)] for p, q in zip(first, second)],
        [[(core, 1, half_rows)], [(far_y, 0, half_rows)]] + [[(p, 0, half_rows)] for p in third],
    ]

    halves = column_halves(theirs, [p[0] for tap in received[0][2:] for p in tap], block)
    far_halves = from_partner(halves, "dp", 0)
    latent, halves = after((latent, halves))
    forward = functools.partial(forward_chunk, idx=idx, tokens=tokens, latent=latent)
    forward = functools.partial(forward, weight=block_weight, right=right_factor, cotangent=out_cotangent)
    act, near_grad, near_out, near_local, near_latent = forward(
        0, remote=received[0], act_before=None, packed=0
    )
    far_near_grad = from_partner(after(near_grad, far_halves), "dp", 0)
    near_terms = over_high_terms(near_out, far_y)
    far_y_half = from_partner(after(far_half, far_y, third, near_grad), "mp", 1)
    act, grad, far_out, far_local, far_latent_term = forward(
        1, remote=received[1], act_before=act, packed=len(high_bits)
    )
    far_far_grad = from_partner(grad, "dp", 0)
    local = [near_local, far_local]
    grads = [near_grad, grad, far_near_grad, far_far_grad]

    def low_grad(a, b):
        return halved_sum(jnp.split(halved_sum([a, b], 0), 2, axis=0), 1)

    def high_grad(part, *terms):
        return high_sum(part), [from_partner(t, "mp", bit) for bit, t in enumerate(terms)]

    def gather_grad(quarter_sum, far_quarter, core_term, y_term, far_half, tokens, remote, grads):
        remote = with_places(remote, near_places)
        near = near_weight_grads(idx, tokens, remote, grads, taps, block)
        stack = jnp.concatenate([quarter_sum, far_quarter], axis=1)
        other = from_partner(stack, "mp", 1)
        core_term = from_partner(core_term, "mp", 0)
        far_core = from_partner(after(far_half, core_term), "mp", 0)
        y_term = from_partner(after(y_term, other, far_core), "mp", 1)
        stack = jnp.concatenate([stack, other], axis=0)
        stack = jnp.concatenate([stack, from_partner(after(stack, far_core), "mp", 0)], axis=0)
        return stack, core_term, y_term, far_core, near

    low_sum = one_step(low_grad, near_latent, far_latent_term)
    low_sum, near_terms, far_near_grad, far_y_half = after(
        (low_sum, near_terms, far_near_grad, far_y_half)
    )
    quarter_sum, low_terms = one_step(high_grad, low_sum, *near_out[:2])
    near_terms = low_terms + near_terms
    far_terms = over_high_terms(far_out, quarter_sum)
    remote = [a + b for a, b in zip(*received)]
    near_places = [[p[1:] for p in tap] for tap in remote]
    gathered_both, core_term, y_term, far_core, near = one_step(
        gather_grad,
        quarter_sum,
        far_quarter,
        *far_out[:2],
        far_half,
        tokens,
        [[p[0] for p in tap] for tap in remote],
        grads[:2],
    )
    far_terms = [core_term, y_term] + far_terms

    far_remote = [[(c, 0, rows)] for c in (far_core, far_y_half)]
    far_remote += [[(far_halves, k, half_rows)] for k in range(len(high_bits))]

    def last_part(gathered_both, far_tokens, near, grads, latent, far_remote):
        far_latent_grad = from_partner(gathered_both[:, :1], "dp", 0)
        far_remote = with_places(far_remote, far_places)
        weights = weight_grads(
            idx, near, far_tokens, far_remote, grads, (latent, 0), (gathered_both, 1), taps, block
        )
        return far_latent_grad, *weights

    far_places = [[p[1:] for p in tap] for tap in far_remote]
    input_grad = input_grads(
        idx, local, list(zip(near_terms, far_terms)), left_factor, (gathered_both, 0), block
    )
    gathered_both, input_grad = after((gathered_both, input_grad))
    far_latent_grad, weight_grad, right_grad = one_step(
        last_part,
        gathered_both,
        far_tokens,
        near,
        grads,
        latent,
        [[p[0] for p in tap] for tap in far_remote],
    )
    left_grad = left_grads(idx, tokens, far_tokens, (gathered_both, 0), (far_latent_grad, 0), block)
    return act, input_grad, weight_grad, left_grad, right_grad


def flip_groups(blocks, distance):
    full_shape = blocks.shape
    group_count = full_shape[1]
    split_view = blocks.reshape(
        (full_shape[0], group_count // (2 * distance), 2, distance) + full_shape[2:]
    )
    return jnp.flip(split_view, axis=2).reshape(full_shape)


def on_device_general(tokens, block_weight, left_factor, right_factor, out_cotangent):
    tok_rows = tokens.shape[0]
    local_width = tokens.shape[1]
    tap_count = block_weight.shape[0]
    block_size = block_weight.shape[1]
    hidden_local = block_weight.shape[2]
    group_count = local_width // block_size
    local_bits = group_count.bit_length() - 1
    tok_blocks = tokens.reshape(tok_rows, group_count, block_size)
    tap_inputs = [tok_blocks]
    for tap_index in range(1, tap_count):
        level_bit = tap_index - 1
        if level_bit < local_bits:
            tap_inputs.append(flip_groups(tok_blocks, 1 << level_bit))
        else:
            partner = from_partner(tokens, "mp", level_bit - local_bits)
            tap_inputs.append(partner.reshape(tok_rows, group_count, block_size))
    stacked = jnp.stack(tap_inputs, axis=2)
    weight_view = block_weight.reshape(tap_count, block_size, group_count, 2 * block_size)
    butterfly = jnp.einsum("tgkc,kcgh->tgh", stacked, weight_view, preferred_element_type=f32)
    butterfly = butterfly.reshape(tok_rows, hidden_local)
    latent = lax.psum(jnp.dot(tokens, left_factor, preferred_element_type=f32), "mp")
    latent_bf = latent.astype(bf16)
    preact = butterfly + jnp.dot(latent_bf, right_factor, preferred_element_type=f32)
    value, slope = gelu_parts(preact)
    activated = value.astype(bf16)
    grad_pre = (out_cotangent.astype(f32) * slope).astype(bf16)
    latent_term = lax.dot_general(grad_pre, right_factor, NT, preferred_element_type=f32)
    latent_grad = lax.psum(latent_term, "mp").astype(bf16)
    left_part = lax.dot_general(tokens, latent_grad, TN, preferred_element_type=f32)
    right_part = lax.dot_general(latent_bf, grad_pre, TN, preferred_element_type=f32)
    left_sum, right_sum = lax.psum((left_part, right_part), "dp")
    grad_view = grad_pre.reshape(tok_rows, group_count, 2 * block_size)
    spread = jnp.einsum("tgh,kcgh->tgkc", grad_view, weight_view, preferred_element_type=f32)
    input_sum = spread[:, :, 0]
    for tap_index in range(1, tap_count):
        level_bit = tap_index - 1
        piece = spread[:, :, tap_index]
        if level_bit < local_bits:
            input_sum = input_sum + flip_groups(piece, 1 << level_bit)
        else:
            returned = from_partner(
                piece.reshape(tok_rows, local_width), "mp", level_bit - local_bits
            )
            input_sum = input_sum + returned.reshape(tok_rows, group_count, block_size)
    low_rank = lax.dot_general(latent_grad, left_factor, NT, preferred_element_type=f32)
    input_grad = (input_sum.reshape(tok_rows, local_width) + low_rank).astype(bf16)
    partial_value = jnp.einsum("tgkc,tgh->kcgh", stacked, grad_view, preferred_element_type=f32)
    partial_value = partial_value.reshape(tap_count, block_size, hidden_local)
    weight_grad = lax.psum_scatter(partial_value, "dp", scatter_dimension=1, tiled=True).astype(bf16)
    return (activated, input_grad, weight_grad, left_sum.astype(bf16), right_sum.astype(bf16))


def solution(mesh):
    pairs = mesh.shape["dp"] == 2 and mesh.shape["mp"] >= 4
    return jax.shard_map(
        on_device if pairs else on_device_general,
        mesh=mesh,
        in_specs=(P("dp", "mp"), P(None, None, "mp"), P("mp", None), P(None, "mp"), P("dp", "mp")),
        out_specs=(P("dp", "mp"), P("dp", "mp"), P(None, "dp", "mp"), P("mp", None), P(None, "mp")),
        check_vma=False,
    )
```

```python
import functools

import jax
import jax.numpy as jnp
from jax import lax
from jax.experimental import pallas as pl
from jax.experimental.pallas import tpu as pltpu
from jax.sharding import PartitionSpec as P

gelu_scale = 0.7978845608028654
gelu_cubic = 0.044715
f32 = jnp.float32
bf16 = jnp.bfloat16
FORWARD_HINTS = (4, 1 / 16)
WEIGHT_HINT = 1 / 16
INPUT_HINT = 1 / 16
STACK_HINT = 458752
NT = (((1,), (1,)), ((), ()))
TN = (((0,), (0,)), ((), ()))


def from_partner(shard, axis, distance):
    return lax.ppermute(shard, axis, [(i, i ^ 1 << distance) for i in range(lax.axis_size(axis))])


def gelu_parts(preact):
    inner = gelu_scale * (preact + gelu_cubic * preact * preact * preact)
    tangent = jnp.tanh(inner)
    value = 0.5 * preact * (1.0 + tangent)
    slope = 0.5 * (1.0 + tangent) + 0.5 * preact * (1.0 - tangent * tangent) * gelu_scale * (
        1.0 + 3.0 * gelu_cubic * preact * preact
    )
    return (value, slope)


def params(mib=60):
    return pltpu.CompilerParams(vmem_limit_bytes=mib * 1024 * 1024)


def cost(hint, flops, moved):
    return pl.CostEstimate(flops=int(hint * flops), bytes_accessed=int(hint * moved), transcendentals=0)


def rows_of(pieces):
    return pieces[0][...] if len(pieces) == 1 else jnp.concatenate([p[...] for p in pieces], axis=0)


def taken(refs):
    refs = list(refs)
    return lambda n: [refs.pop(0) for _ in range(n)]


def forward_body(local_taps, pieces, aliased, packed, idx_ref, *refs):
    take = taken(refs)
    own = [r[...] for r in take(local_taps)]
    remote_refs = [take(n) for n in pieces]
    remote = [rows_of(r) for r in remote_refs]
    remote_refs = [r[0] for r in remote_refs]
    latent = jnp.concatenate([r[0] for r in take(2)], axis=0)
    weight_ref, right_ref, cot_ref = take(3)
    take(1 if aliased else 0)
    act_ref, grad_ref = take(2)
    terms = take(len(pieces))
    local_ref, latent_term_ref = take(2)
    group = pl.program_id(0)
    taps, block, hidden = weight_ref.shape
    weights = weight_ref[...].reshape(taps * block, hidden)
    right = right_ref[...]
    preact = jnp.dot(jnp.concatenate(own + remote, axis=1), weights, preferred_element_type=f32)
    preact = preact + jnp.dot(latent, right, preferred_element_type=f32)
    value, slope = gelu_parts(preact)
    act_ref[...] = value.astype(bf16)
    grad = (cot_ref[...].astype(f32) * slope).astype(bf16)
    rows = grad.shape[0]
    grad_ref[:rows] = grad
    if packed:
        half = block // 2
        height = grad_ref.shape[0] - rows
        theirs = pl.ds(pl.multiple_of((1 - idx_ref[1]) * half, half), half)
        cells = [
            ref[row : row + height, theirs] for ref in remote_refs[-packed:] for row in range(0, rows, height)
        ]
        grad_ref[rows:] = jnp.concatenate(cells, axis=1)
    spread = lax.dot_general(grad, weights, NT, preferred_element_type=f32)
    for k, term_ref in enumerate(terms):
        lo = (local_taps + k) * block
        term_ref[...] = spread[:, lo : lo + block].astype(bf16)

    @pl.when(group == 0)
    def _():
        local_ref[...] = jnp.zeros_like(local_ref)
        latent_term_ref[...] = jnp.zeros_like(latent_term_ref)

    for k in range(local_taps):
        target = group if k == 0 else group ^ (1 << (k - 1))
        cols = pl.ds(pl.multiple_of(target * block, block), block)
        local_ref[:, cols] += spread[:, k * block : (k + 1) * block]
    latent_term_ref[...] += lax.dot_general(grad, right, NT, preferred_element_type=f32)


def forward_chunk(chunk, idx, tokens, remote, latent, weight, right, cotangent, act_before, packed):
    taps, block, hidden_local = weight.shape
    width = tokens.shape[1]
    rows = tokens.shape[0] // 2
    groups = width // block
    hidden = hidden_local // groups
    local_taps = taps - len(remote)
    quarter, rank = latent.shape[2:]
    height = packed * rows * (block // 2) // hidden
    own_spec = lambda k: pl.BlockSpec(
        (rows, block), lambda g, idx: (chunk, g if k == 0 else g ^ (1 << (k - 1)))
    )
    piece_spec = lambda piece: pl.BlockSpec((piece[2], block), lambda g, idx: (piece[1], g))
    latent_spec = lambda k: pl.BlockSpec(
        (1, None, quarter, rank), lambda g, idx: (idx[0] ^ k, 0, 0, 0)
    )
    in_specs = [own_spec(k) for k in range(local_taps)]
    in_specs += [piece_spec(p) for tap in remote for p in tap]
    in_specs += [latent_spec(2 * chunk), latent_spec(2 * chunk + 1)]
    in_specs += [
        pl.BlockSpec((taps, block, hidden), lambda g, idx: (0, 0, g)),
        pl.BlockSpec((rank, hidden), lambda g, idx: (0, g)),
        pl.BlockSpec((rows, hidden), lambda g, idx: (chunk, g)),
    ]
    args = [tokens] * local_taps + [p[0] for tap in remote for p in tap]
    args += [latent, latent, weight, right, cotangent]
    aliases = {}
    if act_before is not None:
        in_specs.append(pl.BlockSpec(memory_space=pl.ANY))
        args.append(act_before)
        aliases = {len(args): 0}
    out_specs = [
        pl.BlockSpec((rows, hidden), lambda g, idx: (chunk, g)),
        pl.BlockSpec((rows + height, hidden), lambda g, idx: (0, g)),
    ]
    out_specs += [pl.BlockSpec((rows, block), lambda g, idx: (0, g))] * len(remote)
    out_specs += [
        pl.BlockSpec((rows, width), lambda g, idx: (0, 0)),
        pl.BlockSpec((rows, rank), lambda g, idx: (0, 0)),
    ]
    shape = jax.ShapeDtypeStruct
    out_shape = [shape(cotangent.shape, bf16), shape((rows + height, hidden_local), bf16)]
    out_shape += [shape((rows, width), bf16)] * len(remote)
    out_shape += [shape((rows, width), f32), shape((rows, rank), f32)]
    outs = pl.pallas_call(
        functools.partial(
            forward_body, local_taps, [len(t) for t in remote], act_before is not None, packed
        ),
        grid_spec=pltpu.PrefetchScalarGridSpec(
            num_scalar_prefetch=1, grid=(groups,), in_specs=in_specs, out_specs=out_specs
        ),
        out_shape=out_shape,
        input_output_aliases=aliases,
        compiler_params=params(),
        cost_estimate=cost(
            FORWARD_HINTS[chunk],
            4 * rows * hidden_local * (taps * block + rank),
            2 * (weight.size + right.size + 3 * rows * hidden_local + 12 * rows * width),
        ),
        name="forward_chunk",
    )(idx, *args)
    act, grad = outs[:2]
    return act, grad, outs[2 : 2 + len(remote)], outs[-2], outs[-1]


def halves_body(idx_ref, *refs):
    row, out_ref = 0, refs[-1]
    for src in refs[:-1]:
        out_ref[row : row + src.shape[0]] = src[...]
        row += src.shape[0]


def column_halves(which, arrays, block):
    width = arrays[0].shape[1]
    half = block // 2
    rows = sum(a.shape[0] for a in arrays)
    return pl.pallas_call(
        halves_body,
        grid_spec=pltpu.PrefetchScalarGridSpec(
            num_scalar_prefetch=1,
            grid=(width // block,),
            in_specs=[
                pl.BlockSpec((a.shape[0], half), lambda j, which: (0, 2 * j + which[0])) for a in arrays
            ],
            out_specs=pl.BlockSpec((rows, half), lambda j, which: (0, j)),
        ),
        out_shape=jax.ShapeDtypeStruct((rows, width // 2), bf16),
        compiler_params=params(8),
        cost_estimate=cost(1 / 16, 0, 2 * rows * width),
        name="column_halves",
    )(which, *arrays)


def in_dp_order(idx_ref, near, far):
    first = idx_ref[1] == 0
    return jnp.concatenate([jnp.where(first, near, far), jnp.where(first, far, near)], axis=0)


def weights_body(local_taps, pieces, far_pieces, packed, idx_ref, *refs):
    take = taken(refs)
    own = [r[...] for r in take(local_taps)]
    remote = [rows_of(take(n)) for n in pieces]
    far_own = [r[...] for r in take(local_taps)]
    far_remote = [rows_of(take(n)) for n in far_pieces]
    pack_ref = take(1)[0]
    half = far_own[0].shape[1]
    cells = [pack_ref[:, lo : lo + half] for lo in range(0, pack_ref.shape[1], half)]
    count = len(cells) // packed
    for k in range(packed):
        tap = len(far_remote) - packed + k
        far_remote[tap] = jnp.concatenate([far_remote[tap]] + cells[k * count : (k + 1) * count], axis=0)
    grad, far_grad = rows_of(take(2)), rows_of(take(2))
    latent_ref, far_latent_ref, weight_ref, right_ref = take(4)
    total = lax.dot_general(jnp.concatenate(own + remote, axis=1), grad, TN, preferred_element_type=f32)
    total = total + lax.dot_general(
        jnp.concatenate(far_own + far_remote, axis=1), far_grad, TN, preferred_element_type=f32
    )
    weight_ref[...] = total.reshape(weight_ref.shape).astype(bf16)
    order = [k ^ idx_ref[0] for k in range(latent_ref.shape[0])]
    latent = jnp.concatenate([latent_ref[k] for k in order], axis=0)
    far_latent = jnp.concatenate([far_latent_ref[k] for k in order], axis=0)
    latents, grads = in_dp_order(idx_ref, latent, far_latent), in_dp_order(idx_ref, grad, far_grad)
    right = lax.dot_general(latents, grads, TN, preferred_element_type=f32)
    right_ref[...] = right.astype(bf16)


def weight_grads(idx, tokens, remote, far_tokens, far_remote, grads, latent, far_latent, taps, block):
    rows, width = tokens.shape
    chunk_rows, hidden_local = grads[0].shape
    groups = width // block
    half = block // 2
    hidden = hidden_local // groups
    local_taps = taps - len(remote)
    rank = latent[0].shape[3]
    pack = grads[-1]
    height = pack.shape[0] - chunk_rows
    packed = height * hidden // (chunk_rows * half)
    own_spec = lambda k: pl.BlockSpec(
        (rows, half), lambda g, idx: (0, 2 * (g if k == 0 else g ^ (1 << (k - 1))) + idx[1])
    )
    own_specs = [own_spec(k) for k in range(local_taps)]
    near_spec = lambda p: pl.BlockSpec((p[2], half), lambda g, idx: (p[1], 2 * g + idx[1]))
    far_spec = lambda p: pl.BlockSpec((p[2], half), lambda g, idx: (p[1], g))
    pieces = [p for tap in remote for p in tap]
    far_pieces = [p for tap in far_remote for p in tap]
    return pl.pallas_call(
        functools.partial(
            weights_body, local_taps, [len(t) for t in remote], [len(t) for t in far_remote], packed
        ),
        grid_spec=pltpu.PrefetchScalarGridSpec(
            num_scalar_prefetch=1,
            grid=(groups,),
            in_specs=own_specs
            + [near_spec(p) for p in pieces]
            + own_specs
            + [far_spec(p) for p in far_pieces]
            + [pl.BlockSpec((height, hidden), lambda g, idx: (chunk_rows // height, g))]
            + [pl.BlockSpec((chunk_rows, hidden), lambda g, idx: (0, g))] * 4
            + [latent_spec(latent), latent_spec(far_latent)],
            out_specs=[
                pl.BlockSpec((taps, half, hidden), lambda g, idx: (0, 0, g)),
                pl.BlockSpec((rank, hidden), lambda g, idx: (0, g)),
            ],
        ),
        out_shape=[
            jax.ShapeDtypeStruct((taps, half, hidden_local), bf16),
            jax.ShapeDtypeStruct((rank, hidden_local), bf16),
        ],
        compiler_params=params(),
        cost_estimate=cost(
            WEIGHT_HINT, 4 * rows * hidden_local * (taps * half + rank), 8 * taps * half * hidden_local
        ),
        name="weight_grads",
    )(
        idx,
        *([tokens] * local_taps),
        *[p[0] for p in pieces],
        *([far_tokens] * local_taps),
        *[p[0] for p in far_pieces],
        pack,
        *grads,
        latent[0],
        far_latent[0],
    )


def stack_body(first_ref, second_ref, out_ref):
    out_ref[:, :1] = first_ref[...]
    out_ref[:, 1:] = second_ref[...]


def stacked(first, second):
    return pl.pallas_call(
        stack_body,
        out_shape=jax.ShapeDtypeStruct((first.shape[0], 2) + first.shape[2:], bf16),
        cost_estimate=cost(STACK_HINT, first.size, 4 * first.size),
        name="stacked",
    )(first, second)


def inputs_body(n_terms, idx_ref, *refs):
    take = taken(refs)
    total = rows_of(take(2))
    for _ in range(n_terms):
        total = total + rows_of(take(2)).astype(f32)
    left_ref, latent_ref, far_latent_ref, tokens_ref, far_tokens_ref, input_ref, left_grad_ref = take(7)
    order = [k ^ idx_ref[0] for k in range(latent_ref.shape[0])]
    latent = jnp.concatenate([latent_ref[k] for k in order], axis=0)
    far_latent = jnp.concatenate([far_latent_ref[k] for k in order], axis=0)
    low_rank = lax.dot_general(latent, left_ref[...], NT, preferred_element_type=f32)
    input_ref[...] = (total + low_rank).astype(bf16)
    tokens = in_dp_order(idx_ref, tokens_ref[...], far_tokens_ref[...])
    latents = in_dp_order(idx_ref, latent, far_latent)
    left = lax.dot_general(tokens, latents, TN, preferred_element_type=f32)
    left_grad_ref[...] = left.astype(bf16)


def latent_spec(pair):
    return pl.BlockSpec(
        (pair[0].shape[0], None) + pair[0].shape[2:], lambda g, idx: (0, pair[1], 0, 0)
    )


def input_grads(idx, local, terms, left, latent, far_latent, tokens, far_tokens, block):
    width, rank = left.shape
    chunk_rows = local[0].shape[0]
    rows = 2 * chunk_rows
    chunk_spec = pl.BlockSpec((chunk_rows, block), lambda g, idx: (0, g))
    token_spec = pl.BlockSpec((rows, block), lambda g, idx: (0, g))
    left_spec = pl.BlockSpec((block, rank), lambda g, idx: (g, 0))
    return pl.pallas_call(
        functools.partial(inputs_body, len(terms)),
        grid_spec=pltpu.PrefetchScalarGridSpec(
            num_scalar_prefetch=1,
            grid=(width // block,),
            in_specs=[chunk_spec] * (2 + 2 * len(terms))
            + [left_spec, latent_spec(latent), latent_spec(far_latent), token_spec, token_spec],
            out_specs=[token_spec, left_spec],
        ),
        out_shape=[
            jax.ShapeDtypeStruct((rows, width), bf16),
            jax.ShapeDtypeStruct((width, rank), bf16),
        ],
        compiler_params=params(),
        cost_estimate=cost(INPUT_HINT, 6 * rows * width * rank, 20 * rows * width),
        name="input_grads",
    )(
        idx,
        *local,
        *[c for pair in terms for c in pair],
        left,
        latent[0],
        far_latent[0],
        tokens,
        far_tokens,
    )


def after(value, *first):
    return lax.optimization_barrier((value, first))[0]


def one_step(f, *args):
    shapes = jax.eval_shape(f, *args)
    other = lambda *_: jax.tree.map(lambda x: jnp.zeros(x.shape, x.dtype), shapes)
    return lax.cond(lax.axis_index("mp") >= 0, f, other, *args)


def halved_sum(halves, bit):
    mine = (lax.axis_index("mp") >> bit) & 1
    sent = jnp.where(mine == 0, halves[1], halves[0])
    kept = jnp.where(mine == 0, halves[0], halves[1])
    return kept + from_partner(sent, "mp", bit)


def high_sum(part):
    for bit in range(2, lax.axis_size("mp").bit_length() - 1):
        part = part + from_partner(part, "mp", bit)
    return part.astype(bf16)[None, None]


def gathered(stack):
    for bit in (1, 0):
        stack = jnp.concatenate([stack, from_partner(stack, "mp", bit)], axis=0)
    return stack


def with_places(arrays, places):
    return [[(a, *p) for a, p in zip(*tap)] for tap in zip(arrays, places)]


def over_high_terms(terms, *first):
    return [from_partner(after(t, *first), "mp", bit) for bit, t in enumerate(terms) if bit >= 2]


def on_device(tokens, block_weight, left_factor, right_factor, out_cotangent):
    rows, width = tokens.shape
    taps, block, _ = block_weight.shape
    groups = width // block
    local_bits = groups.bit_length() - 1
    high_bits = range(2, taps - 1 - local_bits)
    mp_index = lax.axis_index("mp")
    dp_index = lax.axis_index("dp")
    place = 2 * (mp_index & 1) + ((mp_index >> 1) & 1)
    idx = jnp.stack([place, dp_index]).astype(jnp.int32)
    mine = dp_index.reshape(1).astype(jnp.int32)
    theirs = 1 - mine
    half_rows = rows // 2

    over_high = lambda x: [from_partner(x, "mp", bit) for bit in high_bits]
    cut = half_rows // 2
    first = over_high(tokens[:cut])

    def low_part(tokens, left):
        part = jnp.dot(tokens, left, preferred_element_type=f32)
        part = halved_sum(jnp.split(part, 2, axis=0), 0)
        core = from_partner(after(tokens, part), "mp", 0)
        return halved_sum(jnp.split(part, 2, axis=0), 1), core

    def high_part(part, tokens):
        far_tokens = from_partner(tokens, "dp", 0)
        near_y = from_partner(tokens[:half_rows], "mp", 1)
        quarter_sum = high_sum(part)
        second = over_high(after(tokens[cut:half_rows], quarter_sum))
        far = from_partner(quarter_sum, "dp", 0)
        far_half = column_halves(mine, [far_tokens], block)
        rest = after(tokens, quarter_sum)[half_rows:]
        return gathered(quarter_sum), far, far_tokens, far_half, near_y, second, rest

    low_sum, core = one_step(low_part, tokens, left_factor)
    low_sum, first = after((low_sum, first))
    latent, far_quarter, far_tokens, far_half, near_y, second, rest = one_step(
        high_part, low_sum, tokens
    )
    third = over_high(rest)
    far_y = from_partner(rest, "mp", 1)
    received = [
        [[(core, 0, half_rows)], [(near_y, 0, half_rows)]]
        + [[(p, 0, cut), (q, 0, half_rows - cut)] for p, q in zip(first, second)],
        [[(core, 1, half_rows)], [(far_y, 0, half_rows)]] + [[(p, 0, half_rows)] for p in third],
    ]

    halves = column_halves(theirs, [p[0] for tap in received[0][2:] for p in tap], block)
    far_halves = from_partner(halves, "dp", 0)
    latent, halves = after((latent, halves))
    forward = functools.partial(forward_chunk, idx=idx, tokens=tokens, latent=latent)
    forward = functools.partial(forward, weight=block_weight, right=right_factor, cotangent=out_cotangent)
    act, near_grad, near_out, near_local, near_latent = forward(
        0, remote=received[0], act_before=None, packed=0
    )
    far_near_grad = from_partner(after(near_grad, far_halves), "dp", 0)
    near_terms = over_high_terms(near_out, far_y)
    far_y_half = from_partner(after(far_half, far_y, third, near_grad), "mp", 1)
    act, grad, far_out, far_local, far_latent_term = forward(
        1, remote=received[1], act_before=act, packed=len(high_bits)
    )
    far_far_grad = from_partner(grad, "dp", 0)
    local = [near_local, far_local]
    grads = [near_grad, grad, far_near_grad, far_far_grad]

    def low_grad(a, b):
        return halved_sum(jnp.split(halved_sum([a, b], 0), 2, axis=0), 1)

    def high_grad(part, *terms):
        return high_sum(part), [from_partner(t, "mp", bit) for bit, t in enumerate(terms)]

    def gather_grad(stack, core_term, far_half):
        core_term = from_partner(core_term, "mp", 0)
        far_core = from_partner(after(far_half, core_term), "mp", 0)
        stack = jnp.concatenate([stack, from_partner(stack, "mp", 1)], axis=0)
        stack = jnp.concatenate([stack, from_partner(after(stack, far_core), "mp", 0)], axis=0)
        return stack, core_term, far_core

    low_sum = one_step(low_grad, near_latent, far_latent_term)
    low_sum, near_terms, far_near_grad, far_y_half = after(
        (low_sum, near_terms, far_near_grad, far_y_half)
    )
    quarter_sum, low_terms = one_step(high_grad, low_sum, *near_out[:2])
    near_terms = low_terms + near_terms
    far_terms = over_high_terms(far_out, quarter_sum)
    gathered_both, core_term, far_core = one_step(
        gather_grad, stacked(quarter_sum, far_quarter), far_out[0], far_half
    )

    def last_part(gathered_both, y_term, tokens, remote, far_tokens, far_remote, grads, latent):
        far_latent_grad = from_partner(gathered_both[:, :1], "dp", 0)
        y_term = from_partner(y_term, "mp", 1)
        weights = weight_grads(
            idx,
            tokens,
            with_places(remote, near_places),
            far_tokens,
            with_places(far_remote, far_places),
            grads,
            (latent, 0),
            (gathered_both, 1),
            taps,
            block,
        )
        return far_latent_grad, y_term, *weights

    remote = [a + b for a, b in zip(*received)]
    far_remote = [[(c, 0, rows)] for c in (far_core, far_y_half)]
    far_remote += [[(far_halves, k, half_rows)] for k in range(len(high_bits))]
    near_places, far_places = [[[p[1:] for p in tap] for tap in r] for r in (remote, far_remote)]
    remote, far_remote = [[[p[0] for p in tap] for tap in r] for r in (remote, far_remote)]
    far_latent_grad, y_term, weight_grad, right_grad = one_step(
        last_part, gathered_both, far_out[1], tokens, remote, far_tokens, far_remote, grads, latent
    )
    far_terms = [core_term, y_term] + far_terms
    input_grad, left_grad = input_grads(
        idx,
        local,
        list(zip(near_terms, far_terms)),
        left_factor,
        (gathered_both, 0),
        (far_latent_grad, 0),
        tokens,
        far_tokens,
        block,
    )
    return act, input_grad, weight_grad, left_grad, right_grad


def flip_groups(blocks, distance):
    full_shape = blocks.shape
    group_count = full_shape[1]
    split_view = blocks.reshape(
        (full_shape[0], group_count // (2 * distance), 2, distance) + full_shape[2:]
    )
    return jnp.flip(split_view, axis=2).reshape(full_shape)


def on_device_general(tokens, block_weight, left_factor, right_factor, out_cotangent):
    tok_rows = tokens.shape[0]
    local_width = tokens.shape[1]
    tap_count = block_weight.shape[0]
    block_size = block_weight.shape[1]
    hidden_local = block_weight.shape[2]
    group_count = local_width // block_size
    local_bits = group_count.bit_length() - 1
    tok_blocks = tokens.reshape(tok_rows, group_count, block_size)
    tap_inputs = [tok_blocks]
    for tap_index in range(1, tap_count):
        level_bit = tap_index - 1
        if level_bit < local_bits:
            tap_inputs.append(flip_groups(tok_blocks, 1 << level_bit))
        else:
            partner = from_partner(tokens, "mp", level_bit - local_bits)
            tap_inputs.append(partner.reshape(tok_rows, group_count, block_size))
    stacked = jnp.stack(tap_inputs, axis=2)
    weight_view = block_weight.reshape(tap_count, block_size, group_count, 2 * block_size)
    butterfly = jnp.einsum("tgkc,kcgh->tgh", stacked, weight_view, preferred_element_type=f32)
    butterfly = butterfly.reshape(tok_rows, hidden_local)
    latent = lax.psum(jnp.dot(tokens, left_factor, preferred_element_type=f32), "mp")
    latent_bf = latent.astype(bf16)
    preact = butterfly + jnp.dot(latent_bf, right_factor, preferred_element_type=f32)
    value, slope = gelu_parts(preact)
    activated = value.astype(bf16)
    grad_pre = (out_cotangent.astype(f32) * slope).astype(bf16)
    latent_term = lax.dot_general(grad_pre, right_factor, NT, preferred_element_type=f32)
    latent_grad = lax.psum(latent_term, "mp").astype(bf16)
    left_part = lax.dot_general(tokens, latent_grad, TN, preferred_element_type=f32)
    right_part = lax.dot_general(latent_bf, grad_pre, TN, preferred_element_type=f32)
    left_sum, right_sum = lax.psum((left_part, right_part), "dp")
    grad_view = grad_pre.reshape(tok_rows, group_count, 2 * block_size)
    spread = jnp.einsum("tgh,kcgh->tgkc", grad_view, weight_view, preferred_element_type=f32)
    input_sum = spread[:, :, 0]
    for tap_index in range(1, tap_count):
        level_bit = tap_index - 1
        piece = spread[:, :, tap_index]
        if level_bit < local_bits:
            input_sum = input_sum + flip_groups(piece, 1 << level_bit)
        else:
            returned = from_partner(
                piece.reshape(tok_rows, local_width), "mp", level_bit - local_bits
            )
            input_sum = input_sum + returned.reshape(tok_rows, group_count, block_size)
    low_rank = lax.dot_general(latent_grad, left_factor, NT, preferred_element_type=f32)
    input_grad = (input_sum.reshape(tok_rows, local_width) + low_rank).astype(bf16)
    partial_value = jnp.einsum("tgkc,tgh->kcgh", stacked, grad_view, preferred_element_type=f32)
    partial_value = partial_value.reshape(tap_count, block_size, hidden_local)
    weight_grad = lax.psum_scatter(partial_value, "dp", scatter_dimension=1, tiled=True).astype(bf16)
    return (activated, input_grad, weight_grad, left_sum.astype(bf16), right_sum.astype(bf16))


def solution(mesh):
    pairs = mesh.shape["dp"] == 2 and mesh.shape["mp"] >= 4
    return jax.shard_map(
        on_device if pairs else on_device_general,
        mesh=mesh,
        in_specs=(P("dp", "mp"), P(None, None, "mp"), P("mp", None), P(None, "mp"), P("dp", "mp")),
        out_specs=(P("dp", "mp"), P("dp", "mp"), P(None, "dp", "mp"), P("mp", None), P(None, "mp")),
        check_vma=False,
    )
```

```python
import functools

import jax
import jax.numpy as jnp
from jax import lax
from jax.experimental import pallas as pl
from jax.experimental.pallas import tpu as pltpu
from jax.sharding import PartitionSpec as P

gelu_scale = 0.7978845608028654
gelu_cubic = 0.044715
f32 = jnp.float32
bf16 = jnp.bfloat16
FORWARD_HINTS = (4, 1)
WEIGHT_HINT = 1 / 16
INPUT_HINT = 1 / 16
STACK_HINT = 458752
NT = (((1,), (1,)), ((), ()))
TN = (((0,), (0,)), ((), ()))


def from_partner(shard, axis, distance):
    return lax.ppermute(shard, axis, [(i, i ^ 1 << distance) for i in range(lax.axis_size(axis))])


def gelu_parts(preact):
    inner = gelu_scale * (preact + gelu_cubic * preact * preact * preact)
    tangent = jnp.tanh(inner)
    value = 0.5 * preact * (1.0 + tangent)
    slope = 0.5 * (1.0 + tangent) + 0.5 * preact * (1.0 - tangent * tangent) * gelu_scale * (
        1.0 + 3.0 * gelu_cubic * preact * preact
    )
    return (value, slope)


def params(mib=60):
    return pltpu.CompilerParams(vmem_limit_bytes=mib * 1024 * 1024)


def cost(hint, flops, moved):
    return pl.CostEstimate(flops=int(hint * flops), bytes_accessed=int(hint * moved), transcendentals=0)


def rows_of(pieces):
    return pieces[0][...] if len(pieces) == 1 else jnp.concatenate([p[...] for p in pieces], axis=0)


def taken(refs):
    refs = list(refs)
    return lambda n: [refs.pop(0) for _ in range(n)]


def forward_body(local_taps, pieces, aliased, packed, idx_ref, *refs):
    take = taken(refs)
    own = [r[...] for r in take(local_taps)]
    remote_refs = [take(n) for n in pieces]
    remote = [rows_of(r) for r in remote_refs]
    remote_refs = [r[0] for r in remote_refs]
    latent = jnp.concatenate([r[0] for r in take(2)], axis=0)
    weight_ref, right_ref, cot_ref = take(3)
    take(1 if aliased else 0)
    act_ref, grad_ref = take(2)
    terms = take(len(pieces))
    local_ref, latent_term_ref = take(2)
    group = pl.program_id(0)
    taps, block, hidden = weight_ref.shape
    weights = weight_ref[...].reshape(taps * block, hidden)
    right = right_ref[...]
    preact = jnp.dot(jnp.concatenate(own + remote, axis=1), weights, preferred_element_type=f32)
    preact = preact + jnp.dot(latent, right, preferred_element_type=f32)
    value, slope = gelu_parts(preact)
    act_ref[...] = value.astype(bf16)
    grad = (cot_ref[...].astype(f32) * slope).astype(bf16)
    rows = grad.shape[0]
    grad_ref[:rows] = grad
    if packed:
        half = block // 2
        height = grad_ref.shape[0] - rows
        theirs = pl.ds(pl.multiple_of((1 - idx_ref[1]) * half, half), half)
        cells = [
            ref[row : row + height, theirs] for ref in remote_refs[-packed:] for row in range(0, rows, height)
        ]
        grad_ref[rows:] = jnp.concatenate(cells, axis=1)
    spread = lax.dot_general(grad, weights, NT, preferred_element_type=f32)
    for k, term_ref in enumerate(terms):
        lo = (local_taps + k) * block
        term_ref[...] = spread[:, lo : lo + block].astype(bf16)

    @pl.when(group == 0)
    def _():
        local_ref[...] = jnp.zeros_like(local_ref)
        latent_term_ref[...] = jnp.zeros_like(latent_term_ref)

    for k in range(local_taps):
        target = group if k == 0 else group ^ (1 << (k - 1))
        cols = pl.ds(pl.multiple_of(target * block, block), block)
        local_ref[:, cols] += spread[:, k * block : (k + 1) * block]
    latent_term_ref[...] += lax.dot_general(grad, right, NT, preferred_element_type=f32)


def forward_chunk(chunk, idx, tokens, remote, latent, weight, right, cotangent, act_before, packed):
    taps, block, hidden_local = weight.shape
    width = tokens.shape[1]
    rows = tokens.shape[0] // 2
    groups = width // block
    hidden = hidden_local // groups
    local_taps = taps - len(remote)
    quarter, rank = latent.shape[2:]
    height = packed * rows * (block // 2) // hidden
    own_spec = lambda k: pl.BlockSpec(
        (rows, block), lambda g, idx: (chunk, g if k == 0 else g ^ (1 << (k - 1)))
    )
    piece_spec = lambda piece: pl.BlockSpec((piece[2], block), lambda g, idx: (piece[1], g))
    latent_spec = lambda k: pl.BlockSpec(
        (1, None, quarter, rank), lambda g, idx: (idx[0] ^ k, 0, 0, 0)
    )
    in_specs = [own_spec(k) for k in range(local_taps)]
    in_specs += [piece_spec(p) for tap in remote for p in tap]
    in_specs += [latent_spec(2 * chunk), latent_spec(2 * chunk + 1)]
    in_specs += [
        pl.BlockSpec((taps, block, hidden), lambda g, idx: (0, 0, g)),
        pl.BlockSpec((rank, hidden), lambda g, idx: (0, g)),
        pl.BlockSpec((rows, hidden), lambda g, idx: (chunk, g)),
    ]
    args = [tokens] * local_taps + [p[0] for tap in remote for p in tap]
    args += [latent, latent, weight, right, cotangent]
    aliases = {}
    if act_before is not None:
        in_specs.append(pl.BlockSpec(memory_space=pl.ANY))
        args.append(act_before)
        aliases = {len(args): 0}
    out_specs = [
        pl.BlockSpec((rows, hidden), lambda g, idx: (chunk, g)),
        pl.BlockSpec((rows + height, hidden), lambda g, idx: (0, g)),
    ]
    out_specs += [pl.BlockSpec((rows, block), lambda g, idx: (0, g))] * len(remote)
    out_specs += [
        pl.BlockSpec((rows, width), lambda g, idx: (0, 0)),
        pl.BlockSpec((rows, rank), lambda g, idx: (0, 0)),
    ]
    shape = jax.ShapeDtypeStruct
    out_shape = [shape(cotangent.shape, bf16), shape((rows + height, hidden_local), bf16)]
    out_shape += [shape((rows, width), bf16)] * len(remote)
    out_shape += [shape((rows, width), f32), shape((rows, rank), f32)]
    outs = pl.pallas_call(
        functools.partial(
            forward_body, local_taps, [len(t) for t in remote], act_before is not None, packed
        ),
        grid_spec=pltpu.PrefetchScalarGridSpec(
            num_scalar_prefetch=1, grid=(groups,), in_specs=in_specs, out_specs=out_specs
        ),
        out_shape=out_shape,
        input_output_aliases=aliases,
        compiler_params=params(),
        cost_estimate=cost(
            FORWARD_HINTS[chunk],
            4 * rows * hidden_local * (taps * block + rank),
            2 * (weight.size + right.size + 3 * rows * hidden_local + 12 * rows * width),
        ),
        name="forward_chunk",
    )(idx, *args)
    act, grad = outs[:2]
    return act, grad, outs[2 : 2 + len(remote)], outs[-2], outs[-1]


def halves_body(block, which, *refs):
    row, out_ref = 0, refs[-1]
    half = block // 2
    for src in refs[:-1]:
        rows, width = src.shape
        for j in range(width // block):
            cols = pl.ds(pl.multiple_of(j * block + which[0] * half, half), half)
            out_ref[row : row + rows, j * half : (j + 1) * half] = src[:, cols]
        row += rows


def column_halves(which, arrays, block):
    width = arrays[0].shape[1]
    rows = sum(a.shape[0] for a in arrays)
    return pl.pallas_call(
        functools.partial(halves_body, block),
        in_specs=[pl.BlockSpec(memory_space=pltpu.SMEM)]
        + [pl.BlockSpec(a.shape, lambda: (0, 0)) for a in arrays],
        out_shape=jax.ShapeDtypeStruct((rows, width // 2), bf16),
        compiler_params=params(8),
        cost_estimate=cost(1 / 16, 0, 2 * rows * width),
        name="column_halves",
    )(which, *arrays)


def in_dp_order(idx_ref, near, far):
    first = idx_ref[1] == 0
    return jnp.concatenate([jnp.where(first, near, far), jnp.where(first, far, near)], axis=0)


def weights_body(local_taps, pieces, far_pieces, packed, idx_ref, *refs):
    take = taken(refs)
    own = [r[...] for r in take(local_taps)]
    remote = [rows_of(take(n)) for n in pieces]
    far_own = [r[...] for r in take(local_taps)]
    far_remote = [rows_of(take(n)) for n in far_pieces]
    pack_ref = take(1)[0]
    half = far_own[0].shape[1]
    cells = [pack_ref[:, lo : lo + half] for lo in range(0, pack_ref.shape[1], half)]
    count = len(cells) // packed
    for k in range(packed):
        tap = len(far_remote) - packed + k
        far_remote[tap] = jnp.concatenate([far_remote[tap]] + cells[k * count : (k + 1) * count], axis=0)
    grad, far_grad = rows_of(take(2)), rows_of(take(2))
    latent_ref, far_latent_ref, weight_ref, right_ref = take(4)
    total = lax.dot_general(jnp.concatenate(own + remote, axis=1), grad, TN, preferred_element_type=f32)
    total = total + lax.dot_general(
        jnp.concatenate(far_own + far_remote, axis=1), far_grad, TN, preferred_element_type=f32
    )
    weight_ref[...] = total.reshape(weight_ref.shape).astype(bf16)
    order = [k ^ idx_ref[0] for k in range(latent_ref.shape[0])]
    latent = jnp.concatenate([latent_ref[k] for k in order], axis=0)
    far_latent = jnp.concatenate([far_latent_ref[k] for k in order], axis=0)
    latents, grads = in_dp_order(idx_ref, latent, far_latent), in_dp_order(idx_ref, grad, far_grad)
    right = lax.dot_general(latents, grads, TN, preferred_element_type=f32)
    right_ref[...] = right.astype(bf16)


def weight_grads(idx, tokens, remote, far_tokens, far_remote, grads, latent, far_latent, taps, block):
    rows, width = tokens.shape
    chunk_rows, hidden_local = grads[0].shape
    groups = width // block
    half = block // 2
    hidden = hidden_local // groups
    local_taps = taps - len(remote)
    rank = latent[0].shape[3]
    pack = grads[-1]
    height = pack.shape[0] - chunk_rows
    packed = height * hidden // (chunk_rows * half)
    own_spec = lambda k: pl.BlockSpec(
        (rows, half), lambda g, idx: (0, 2 * (g if k == 0 else g ^ (1 << (k - 1))) + idx[1])
    )
    own_specs = [own_spec(k) for k in range(local_taps)]
    near_spec = lambda p: pl.BlockSpec((p[2], half), lambda g, idx: (p[1], 2 * g + idx[1]))
    far_spec = lambda p: pl.BlockSpec((p[2], half), lambda g, idx: (p[1], g))
    pieces = [p for tap in remote for p in tap]
    far_pieces = [p for tap in far_remote for p in tap]
    return pl.pallas_call(
        functools.partial(
            weights_body, local_taps, [len(t) for t in remote], [len(t) for t in far_remote], packed
        ),
        grid_spec=pltpu.PrefetchScalarGridSpec(
            num_scalar_prefetch=1,
            grid=(groups,),
            in_specs=own_specs
            + [near_spec(p) for p in pieces]
            + own_specs
            + [far_spec(p) for p in far_pieces]
            + [pl.BlockSpec((height, hidden), lambda g, idx: (chunk_rows // height, g))]
            + [pl.BlockSpec((chunk_rows, hidden), lambda g, idx: (0, g))] * 4
            + [latent_spec(latent), latent_spec(far_latent)],
            out_specs=[
                pl.BlockSpec((taps, half, hidden), lambda g, idx: (0, 0, g)),
                pl.BlockSpec((rank, hidden), lambda g, idx: (0, g)),
            ],
        ),
        out_shape=[
            jax.ShapeDtypeStruct((taps, half, hidden_local), bf16),
            jax.ShapeDtypeStruct((rank, hidden_local), bf16),
        ],
        compiler_params=params(),
        cost_estimate=cost(
            WEIGHT_HINT, 4 * rows * hidden_local * (taps * half + rank), 8 * taps * half * hidden_local
        ),
        name="weight_grads",
    )(
        idx,
        *([tokens] * local_taps),
        *[p[0] for p in pieces],
        *([far_tokens] * local_taps),
        *[p[0] for p in far_pieces],
        pack,
        *grads,
        latent[0],
        far_latent[0],
    )


def stack_body(first_ref, second_ref, out_ref):
    out_ref[:, :1] = first_ref[...]
    out_ref[:, 1:] = second_ref[...]


def stacked(first, second):
    return pl.pallas_call(
        stack_body,
        out_shape=jax.ShapeDtypeStruct((first.shape[0], 2) + first.shape[2:], bf16),
        cost_estimate=cost(STACK_HINT, first.size, 4 * first.size),
        name="stacked",
    )(first, second)


def inputs_body(n_terms, idx_ref, *refs):
    take = taken(refs)
    total = rows_of(take(2))
    for _ in range(n_terms):
        total = total + rows_of(take(2)).astype(f32)
    left_ref, latent_ref, far_latent_ref, tokens_ref, far_tokens_ref = take(5)
    input_ref, left_grad_ref = take(2)
    order = [k ^ idx_ref[0] for k in range(latent_ref.shape[0])]
    latent = jnp.concatenate([latent_ref[k] for k in order], axis=0)
    far_latent = jnp.concatenate([far_latent_ref[k] for k in order], axis=0)
    low_rank = lax.dot_general(latent, left_ref[...], NT, preferred_element_type=f32)
    input_ref[...] = (total + low_rank).astype(bf16)
    tokens = in_dp_order(idx_ref, tokens_ref[...], far_tokens_ref[...])
    latents = in_dp_order(idx_ref, latent, far_latent)
    left = lax.dot_general(tokens, latents, TN, preferred_element_type=f32)
    left_grad_ref[...] = left.astype(bf16)


def latent_spec(pair):
    return pl.BlockSpec(
        (pair[0].shape[0], None) + pair[0].shape[2:], lambda g, idx: (0, pair[1], 0, 0)
    )


def input_grads(idx, local, terms, left, latent, far_latent, tokens, far_tokens, block):
    block = 2 * block
    width, rank = left.shape
    chunk_rows = local[0].shape[0]
    rows = 2 * chunk_rows
    chunk_spec = pl.BlockSpec((chunk_rows, block), lambda g, idx: (0, g))
    token_spec = pl.BlockSpec((rows, block), lambda g, idx: (0, g))
    left_spec = pl.BlockSpec((block, rank), lambda g, idx: (g, 0))
    return pl.pallas_call(
        functools.partial(inputs_body, len(terms)),
        grid_spec=pltpu.PrefetchScalarGridSpec(
            num_scalar_prefetch=1,
            grid=(width // block,),
            in_specs=[chunk_spec] * (2 + 2 * len(terms))
            + [left_spec, latent_spec(latent), latent_spec(far_latent)]
            + [token_spec, token_spec],
            out_specs=[token_spec, left_spec],
        ),
        out_shape=[
            jax.ShapeDtypeStruct((rows, width), bf16),
            jax.ShapeDtypeStruct((width, rank), bf16),
        ],
        compiler_params=params(),
        cost_estimate=cost(INPUT_HINT, 6 * rows * width * rank, 20 * rows * width),
        name="input_grads",
    )(
        idx,
        *local,
        *[c for pair in terms for c in pair],
        left,
        latent[0],
        far_latent[0],
        tokens,
        far_tokens,
    )


def after(value, *first):
    return lax.optimization_barrier((value, first))[0]


def one_step(f, *args):
    shapes = jax.eval_shape(f, *args)
    other = lambda *_: jax.tree.map(lambda x: jnp.zeros(x.shape, x.dtype), shapes)
    return lax.cond(lax.axis_index("mp") >= 0, f, other, *args)


def halved_sum(halves, bit):
    mine = (lax.axis_index("mp") >> bit) & 1
    sent = jnp.where(mine == 0, halves[1], halves[0])
    kept = jnp.where(mine == 0, halves[0], halves[1])
    return kept + from_partner(sent, "mp", bit)


def high_sum(part, first_bit=2):
    for bit in range(first_bit, lax.axis_size("mp").bit_length() - 1):
        part = part + from_partner(part, "mp", bit)
    return part.astype(bf16)[None, None]


def gathered(stack):
    for bit in (1, 0):
        stack = jnp.concatenate([stack, from_partner(stack, "mp", bit)], axis=0)
    return stack


def with_places(arrays, places):
    return [[(a, *p) for a, p in zip(*tap)] for tap in zip(arrays, places)]


def over_high_terms(terms, *first):
    return [from_partner(after(t, *first), "mp", bit) for bit, t in enumerate(terms) if bit >= 2]


def on_device(tokens, block_weight, left_factor, right_factor, out_cotangent):
    rows, width = tokens.shape
    taps, block, _ = block_weight.shape
    groups = width // block
    local_bits = groups.bit_length() - 1
    high_bits = range(2, taps - 1 - local_bits)
    mp_index = lax.axis_index("mp")
    dp_index = lax.axis_index("dp")
    place = 2 * (mp_index & 1) + ((mp_index >> 1) & 1)
    idx = jnp.stack([place, dp_index]).astype(jnp.int32)
    mine = dp_index.reshape(1).astype(jnp.int32)
    theirs = 1 - mine
    half_rows = rows // 2

    over_high = lambda x: [from_partner(x, "mp", bit) for bit in high_bits]
    cut = half_rows // 2
    first = over_high(tokens[:cut])

    def low_part(tokens, left):
        part = jnp.dot(tokens, left, preferred_element_type=f32)
        part = halved_sum(jnp.split(part, 2, axis=0), 0)
        core = from_partner(after(tokens, part), "mp", 0)
        tokens = after(tokens, part)
        slices = [tokens[:half_rows], tokens[cut:half_rows], tokens[half_rows:]]
        return halved_sum(jnp.split(part, 2, axis=0), 1), core, slices

    def high_part(part, tokens, y_rows, rest, first):
        far_tokens = from_partner(tokens, "dp", 0)
        near_y = from_partner(y_rows, "mp", 1)
        stack = high_sum(part)
        second = over_high(after(rest, stack))
        far = from_partner(stack, "dp", 0)
        stack = jnp.concatenate([stack, from_partner(after(stack, near_y), "mp", 1)], axis=0)
        far_half = column_halves(mine, [far_tokens], block)
        stack = jnp.concatenate([stack, from_partner(after(stack, far, far_half), "mp", 0)], axis=0)
        high = [p for pair in zip(first, second) for p in pair]
        return stack, far, far_tokens, far_half, near_y, second, column_halves(theirs, high, block)

    low_sum, core, slices = one_step(low_part, tokens, left_factor)
    low_sum, first = after((low_sum, first))
    latent, far_quarter, far_tokens, far_half, near_y, second, halves = one_step(
        high_part, low_sum, tokens, *slices[:2], first
    )
    rest = after(slices[2], latent)
    third = over_high(rest)
    far_y = from_partner(rest, "mp", 1)
    received = [
        [[(core, 0, half_rows)], [(near_y, 0, half_rows)]]
        + [[(p, 0, cut), (q, 0, half_rows - cut)] for p, q in zip(first, second)],
        [[(core, 1, half_rows)], [(far_y, 0, half_rows)]] + [[(p, 0, half_rows)] for p in third],
    ]

    far_halves = from_partner(halves, "dp", 0)
    forward = functools.partial(forward_chunk, idx=idx, tokens=tokens, latent=latent)
    forward = functools.partial(forward, weight=block_weight, right=right_factor, cotangent=out_cotangent)
    act, near_grad, near_out, near_local, near_latent = forward(
        0, remote=received[0], act_before=None, packed=0
    )
    far_near_grad = from_partner(after(near_grad, far_halves), "dp", 0)
    near_terms = over_high_terms(near_out, far_y)
    far_y_half = from_partner(after(far_half, near_grad, third), "mp", 1)
    act, grad, far_out, far_local, far_latent_term = forward(
        1, remote=received[1], act_before=act, packed=len(high_bits)
    )
    far_far_grad = from_partner(grad, "dp", 0)
    local = [near_local, far_local]
    grads = [near_grad, grad, far_near_grad, far_far_grad]

    def low_grad(a, b):
        return halved_sum(jnp.split(halved_sum([a, b], 0), 2, axis=0), 1)

    def high_grad(part, *terms):
        return high_sum(part), [from_partner(t, "mp", bit) for bit, t in enumerate(terms)]

    def gather_grad(stack, core_term, far_half):
        stack = jnp.concatenate([stack, from_partner(stack, "mp", 1)], axis=0)
        core_term = from_partner(core_term, "mp", 0)
        stack, core_term = after((stack, core_term))
        far_core = from_partner(after(far_half, stack), "mp", 0)
        return jnp.concatenate([stack, from_partner(stack, "mp", 0)], axis=0), core_term, far_core

    near_latent, far_near_grad = after((near_latent, far_near_grad))
    low_sum = one_step(low_grad, near_latent, far_latent_term)
    low_sum, far_y_half, near_terms = after((low_sum, far_y_half, near_terms))
    quarter_sum, low_terms = one_step(high_grad, low_sum, *near_out[:2])
    far_terms = over_high_terms(far_out, quarter_sum)
    near_terms = low_terms + near_terms
    gathered_both, core_term, far_core = one_step(
        gather_grad, stacked(quarter_sum, far_quarter), far_out[0], far_half
    )

    def last_part(gathered_both, y_term, tokens, remote, far_tokens, far_remote, grads, latent):
        far_latent_grad = from_partner(gathered_both[:, :1], "dp", 0)
        y_term = from_partner(y_term, "mp", 1)
        weights = weight_grads(
            idx,
            tokens,
            with_places(remote, near_places),
            far_tokens,
            with_places(far_remote, far_places),
            grads,
            (latent, 0),
            (gathered_both, 1),
            taps,
            block,
        )
        return far_latent_grad, y_term, *weights

    remote = [a + b for a, b in zip(*received)]
    far_remote = [[(c, 0, rows)] for c in (far_core, far_y_half)]
    far_remote += [[(far_halves, k, half_rows)] for k in range(len(high_bits))]
    near_places, far_places = [[[p[1:] for p in tap] for tap in r] for r in (remote, far_remote)]
    remote, far_remote = [[[p[0] for p in tap] for tap in r] for r in (remote, far_remote)]
    far_latent_grad, y_term, weight_grad, right_grad = one_step(
        last_part, gathered_both, far_out[1], tokens, remote, far_tokens, far_remote, grads, latent
    )
    far_terms = [core_term, y_term] + far_terms
    input_grad, left_grad = input_grads(
        idx,
        local,
        list(zip(near_terms, far_terms)),
        left_factor,
        (gathered_both, 0),
        (far_latent_grad, 0),
        tokens,
        far_tokens,
        block,
    )
    return act, input_grad, weight_grad, left_grad, right_grad


def flip_groups(blocks, distance):
    full_shape = blocks.shape
    group_count = full_shape[1]
    split_view = blocks.reshape(
        (full_shape[0], group_count // (2 * distance), 2, distance) + full_shape[2:]
    )
    return jnp.flip(split_view, axis=2).reshape(full_shape)


def on_device_general(tokens, block_weight, left_factor, right_factor, out_cotangent):
    tok_rows = tokens.shape[0]
    local_width = tokens.shape[1]
    tap_count = block_weight.shape[0]
    block_size = block_weight.shape[1]
    hidden_local = block_weight.shape[2]
    group_count = local_width // block_size
    local_bits = group_count.bit_length() - 1
    tok_blocks = tokens.reshape(tok_rows, group_count, block_size)
    tap_inputs = [tok_blocks]
    for tap_index in range(1, tap_count):
        level_bit = tap_index - 1
        if level_bit < local_bits:
            tap_inputs.append(flip_groups(tok_blocks, 1 << level_bit))
        else:
            partner = from_partner(tokens, "mp", level_bit - local_bits)
            tap_inputs.append(partner.reshape(tok_rows, group_count, block_size))
    stacked = jnp.stack(tap_inputs, axis=2)
    weight_view = block_weight.reshape(tap_count, block_size, group_count, 2 * block_size)
    butterfly = jnp.einsum("tgkc,kcgh->tgh", stacked, weight_view, preferred_element_type=f32)
    butterfly = butterfly.reshape(tok_rows, hidden_local)
    latent = lax.psum(jnp.dot(tokens, left_factor, preferred_element_type=f32), "mp")
    latent_bf = latent.astype(bf16)
    preact = butterfly + jnp.dot(latent_bf, right_factor, preferred_element_type=f32)
    value, slope = gelu_parts(preact)
    activated = value.astype(bf16)
    grad_pre = (out_cotangent.astype(f32) * slope).astype(bf16)
    latent_term = lax.dot_general(grad_pre, right_factor, NT, preferred_element_type=f32)
    latent_grad = lax.psum(latent_term, "mp").astype(bf16)
    left_part = lax.dot_general(tokens, latent_grad, TN, preferred_element_type=f32)
    right_part = lax.dot_general(latent_bf, grad_pre, TN, preferred_element_type=f32)
    left_sum, right_sum = lax.psum((left_part, right_part), "dp")
    grad_view = grad_pre.reshape(tok_rows, group_count, 2 * block_size)
    spread = jnp.einsum("tgh,kcgh->tgkc", grad_view, weight_view, preferred_element_type=f32)
    input_sum = spread[:, :, 0]
    for tap_index in range(1, tap_count):
        level_bit = tap_index - 1
        piece = spread[:, :, tap_index]
        if level_bit < local_bits:
            input_sum = input_sum + flip_groups(piece, 1 << level_bit)
        else:
            returned = from_partner(
                piece.reshape(tok_rows, local_width), "mp", level_bit - local_bits
            )
            input_sum = input_sum + returned.reshape(tok_rows, group_count, block_size)
    low_rank = lax.dot_general(latent_grad, left_factor, NT, preferred_element_type=f32)
    input_grad = (input_sum.reshape(tok_rows, local_width) + low_rank).astype(bf16)
    partial_value = jnp.einsum("tgkc,tgh->kcgh", stacked, grad_view, preferred_element_type=f32)
    partial_value = partial_value.reshape(tap_count, block_size, hidden_local)
    weight_grad = lax.psum_scatter(partial_value, "dp", scatter_dimension=1, tiled=True).astype(bf16)
    return (activated, input_grad, weight_grad, left_sum.astype(bf16), right_sum.astype(bf16))


def solution(mesh):
    pairs = mesh.shape["dp"] == 2 and mesh.shape["mp"] >= 4
    return jax.shard_map(
        on_device if pairs else on_device_general,
        mesh=mesh,
        in_specs=(P("dp", "mp"), P(None, None, "mp"), P("mp", None), P(None, "mp"), P("dp", "mp")),
        out_specs=(P("dp", "mp"), P("dp", "mp"), P(None, "dp", "mp"), P("mp", None), P(None, "mp")),
        check_vma=False,
    )
```

```python
import functools

import jax
import jax.numpy as jnp
from jax import lax
from jax.experimental import pallas as pl
from jax.experimental.pallas import tpu as pltpu
from jax.sharding import PartitionSpec as P

gelu_scale = 0.7978845608028654
gelu_cubic = 0.044715
f32 = jnp.float32
bf16 = jnp.bfloat16
FORWARD_HINTS = (4, 1)
WEIGHT_HINT = 1 / 16
INPUT_HINT = 1 / 16
STACK_HINT = 458752
NT = (((1,), (1,)), ((), ()))
TN = (((0,), (0,)), ((), ()))


def from_partner(shard, axis, distance):
    return lax.ppermute(shard, axis, [(i, i ^ 1 << distance) for i in range(lax.axis_size(axis))])


def gelu_parts(preact):
    inner = gelu_scale * (preact + gelu_cubic * preact * preact * preact)
    tangent = jnp.tanh(inner)
    value = 0.5 * preact * (1.0 + tangent)
    slope = 0.5 * (1.0 + tangent) + 0.5 * preact * (1.0 - tangent * tangent) * gelu_scale * (
        1.0 + 3.0 * gelu_cubic * preact * preact
    )
    return (value, slope)


def params(mib=60):
    return pltpu.CompilerParams(vmem_limit_bytes=mib * 1024 * 1024)


def cost(hint, flops, moved):
    return pl.CostEstimate(flops=int(hint * flops), bytes_accessed=int(hint * moved), transcendentals=0)


def rows_of(pieces):
    return pieces[0][...] if len(pieces) == 1 else jnp.concatenate([p[...] for p in pieces], axis=0)


def taken(refs):
    refs = list(refs)
    return lambda n: [refs.pop(0) for _ in range(n)]


def forward_body(local_taps, pieces, aliased, packed, idx_ref, *refs):
    take = taken(refs)
    tokens_ref = take(1)[0]
    remote_refs = [take(n) for n in pieces]
    remote = [rows_of(r) for r in remote_refs]
    remote_refs = [r[0] for r in remote_refs]
    latent = jnp.concatenate([r[0] for r in take(2)], axis=0)
    weight_ref, right_ref, cot_ref = take(3)
    take(1 if aliased else 0)
    act_ref, grad_ref = take(2)
    terms = take(len(pieces))
    local_ref, latent_term_ref = take(2)
    group = pl.program_id(0)
    taps, block, hidden = weight_ref.shape
    flips = [group if k == 0 else group ^ (1 << (k - 1)) for k in range(local_taps)]
    own = [tokens_ref[:, pl.ds(pl.multiple_of(j * block, block), block)] for j in flips]
    weights = weight_ref[...].reshape(taps * block, hidden)
    right = right_ref[...]
    preact = jnp.dot(jnp.concatenate(own + remote, axis=1), weights, preferred_element_type=f32)
    preact = preact + jnp.dot(latent, right, preferred_element_type=f32)
    value, slope = gelu_parts(preact)
    act_ref[...] = value.astype(bf16)
    grad = (cot_ref[...].astype(f32) * slope).astype(bf16)
    rows = grad.shape[0]
    grad_ref[:rows] = grad
    if packed:
        half = block // 2
        height = grad_ref.shape[0] - rows
        theirs = pl.ds(pl.multiple_of((1 - idx_ref[1]) * half, half), half)
        cells = [
            ref[row : row + height, theirs] for ref in remote_refs[-packed:] for row in range(0, rows, height)
        ]
        grad_ref[rows:] = jnp.concatenate(cells, axis=1)
    spread = lax.dot_general(grad, weights, NT, preferred_element_type=f32)
    for k, term_ref in enumerate(terms):
        lo = (local_taps + k) * block
        term_ref[...] = spread[:, lo : lo + block].astype(bf16)

    @pl.when(group == 0)
    def _():
        local_ref[...] = jnp.zeros_like(local_ref)
        latent_term_ref[...] = jnp.zeros_like(latent_term_ref)

    for k in range(local_taps):
        target = group if k == 0 else group ^ (1 << (k - 1))
        cols = pl.ds(pl.multiple_of(target * block, block), block)
        local_ref[:, cols] += spread[:, k * block : (k + 1) * block]
    latent_term_ref[...] += lax.dot_general(grad, right, NT, preferred_element_type=f32)


def forward_chunk(chunk, idx, tokens, remote, latent, weight, right, cotangent, act_before, packed):
    taps, block, hidden_local = weight.shape
    width = tokens.shape[1]
    rows = tokens.shape[0] // 2
    groups = width // block
    hidden = hidden_local // groups
    local_taps = taps - len(remote)
    quarter, rank = latent.shape[2:]
    height = packed * rows * (block // 2) // hidden
    piece_spec = lambda piece: pl.BlockSpec((piece[2], block), lambda g, idx: (piece[1], g))
    latent_spec = lambda k: pl.BlockSpec(
        (1, None, quarter, rank), lambda g, idx: (idx[0] ^ k, 0, 0, 0)
    )
    in_specs = [pl.BlockSpec((rows, width), lambda g, idx: (chunk, 0))]
    in_specs += [piece_spec(p) for tap in remote for p in tap]
    in_specs += [latent_spec(2 * chunk), latent_spec(2 * chunk + 1)]
    in_specs += [
        pl.BlockSpec((taps, block, hidden), lambda g, idx: (0, 0, g)),
        pl.BlockSpec((rank, hidden), lambda g, idx: (0, g)),
        pl.BlockSpec((rows, hidden), lambda g, idx: (chunk, g)),
    ]
    args = [tokens] + [p[0] for tap in remote for p in tap]
    args += [latent, latent, weight, right, cotangent]
    aliases = {}
    if act_before is not None:
        in_specs.append(pl.BlockSpec(memory_space=pl.ANY))
        args.append(act_before)
        aliases = {len(args): 0}
    out_specs = [
        pl.BlockSpec((rows, hidden), lambda g, idx: (chunk, g)),
        pl.BlockSpec((rows + height, hidden), lambda g, idx: (0, g)),
    ]
    out_specs += [pl.BlockSpec((rows, block), lambda g, idx: (0, g))] * len(remote)
    out_specs += [
        pl.BlockSpec((rows, width), lambda g, idx: (0, 0)),
        pl.BlockSpec((rows, rank), lambda g, idx: (0, 0)),
    ]
    shape = jax.ShapeDtypeStruct
    out_shape = [shape(cotangent.shape, bf16), shape((rows + height, hidden_local), bf16)]
    out_shape += [shape((rows, width), bf16)] * len(remote)
    out_shape += [shape((rows, width), f32), shape((rows, rank), f32)]
    outs = pl.pallas_call(
        functools.partial(
            forward_body, local_taps, [len(t) for t in remote], act_before is not None, packed
        ),
        grid_spec=pltpu.PrefetchScalarGridSpec(
            num_scalar_prefetch=1, grid=(groups,), in_specs=in_specs, out_specs=out_specs
        ),
        out_shape=out_shape,
        input_output_aliases=aliases,
        compiler_params=params(),
        cost_estimate=cost(
            FORWARD_HINTS[chunk],
            4 * rows * hidden_local * (taps * block + rank),
            2 * (weight.size + right.size + 3 * rows * hidden_local + 12 * rows * width),
        ),
        name="forward_chunk",
    )(idx, *args)
    act, grad = outs[:2]
    return act, grad, outs[2 : 2 + len(remote)], outs[-2], outs[-1]


def halves_body(block, which, *refs):
    row, out_ref = 0, refs[-1]
    half = block // 2
    for src in refs[:-1]:
        rows, width = src.shape
        for j in range(width // block):
            cols = pl.ds(pl.multiple_of(j * block + which[0] * half, half), half)
            out_ref[row : row + rows, j * half : (j + 1) * half] = src[:, cols]
        row += rows


def column_halves(which, arrays, block):
    width = arrays[0].shape[1]
    rows = sum(a.shape[0] for a in arrays)
    return pl.pallas_call(
        functools.partial(halves_body, block),
        in_specs=[pl.BlockSpec(memory_space=pltpu.SMEM)]
        + [pl.BlockSpec(a.shape, lambda: (0, 0)) for a in arrays],
        out_shape=jax.ShapeDtypeStruct((rows, width // 2), bf16),
        compiler_params=params(8),
        cost_estimate=cost(1 / 16, 0, 2 * rows * width),
        name="column_halves",
    )(which, *arrays)


def in_dp_order(idx_ref, near, far):
    first = idx_ref[1] == 0
    return jnp.concatenate([jnp.where(first, near, far), jnp.where(first, far, near)], axis=0)


def weights_body(local_taps, pieces, far_pieces, packed, idx_ref, *refs):
    take = taken(refs)
    own = [r[...] for r in take(local_taps)]
    remote = [rows_of(take(n)) for n in pieces]
    far_own = [r[...] for r in take(local_taps)]
    far_remote = [rows_of(take(n)) for n in far_pieces]
    pack_ref = take(1)[0]
    half = far_own[0].shape[1]
    cells = [pack_ref[:, lo : lo + half] for lo in range(0, pack_ref.shape[1], half)]
    count = len(cells) // packed
    for k in range(packed):
        tap = len(far_remote) - packed + k
        far_remote[tap] = jnp.concatenate([far_remote[tap]] + cells[k * count : (k + 1) * count], axis=0)
    grad, far_grad = rows_of(take(2)), rows_of(take(2))
    latent_ref, far_latent_ref, weight_ref, right_ref = take(4)
    total = lax.dot_general(jnp.concatenate(own + remote, axis=1), grad, TN, preferred_element_type=f32)
    total = total + lax.dot_general(
        jnp.concatenate(far_own + far_remote, axis=1), far_grad, TN, preferred_element_type=f32
    )
    weight_ref[...] = total.reshape(weight_ref.shape).astype(bf16)
    order = [k ^ idx_ref[0] for k in range(latent_ref.shape[0])]
    latent = jnp.concatenate([latent_ref[k] for k in order], axis=0)
    far_latent = jnp.concatenate([far_latent_ref[k] for k in order], axis=0)
    latents, grads = in_dp_order(idx_ref, latent, far_latent), in_dp_order(idx_ref, grad, far_grad)
    right = lax.dot_general(latents, grads, TN, preferred_element_type=f32)
    right_ref[...] = right.astype(bf16)


def weight_grads(idx, tokens, remote, far_tokens, far_remote, grads, latent, far_latent, taps, block):
    rows, width = tokens.shape
    chunk_rows, hidden_local = grads[0].shape
    groups = width // block
    half = block // 2
    hidden = hidden_local // groups
    local_taps = taps - len(remote)
    rank = latent[0].shape[3]
    pack = grads[-1]
    height = pack.shape[0] - chunk_rows
    packed = height * hidden // (chunk_rows * half)
    own_spec = lambda k: pl.BlockSpec(
        (rows, half), lambda g, idx: (0, 2 * (g if k == 0 else g ^ (1 << (k - 1))) + idx[1])
    )
    own_specs = [own_spec(k) for k in range(local_taps)]
    near_spec = lambda p: pl.BlockSpec((p[2], half), lambda g, idx: (p[1], 2 * g + idx[1]))
    far_spec = lambda p: pl.BlockSpec((p[2], half), lambda g, idx: (p[1], g))
    pieces = [p for tap in remote for p in tap]
    far_pieces = [p for tap in far_remote for p in tap]
    return pl.pallas_call(
        functools.partial(
            weights_body, local_taps, [len(t) for t in remote], [len(t) for t in far_remote], packed
        ),
        grid_spec=pltpu.PrefetchScalarGridSpec(
            num_scalar_prefetch=1,
            grid=(groups,),
            in_specs=own_specs
            + [near_spec(p) for p in pieces]
            + own_specs
            + [far_spec(p) for p in far_pieces]
            + [pl.BlockSpec((height, hidden), lambda g, idx: (chunk_rows // height, g))]
            + [pl.BlockSpec((chunk_rows, hidden), lambda g, idx: (0, g))] * 4
            + [latent_spec(latent), latent_spec(far_latent)],
            out_specs=[
                pl.BlockSpec((taps, half, hidden), lambda g, idx: (0, 0, g)),
                pl.BlockSpec((rank, hidden), lambda g, idx: (0, g)),
            ],
        ),
        out_shape=[
            jax.ShapeDtypeStruct((taps, half, hidden_local), bf16),
            jax.ShapeDtypeStruct((rank, hidden_local), bf16),
        ],
        compiler_params=params(),
        cost_estimate=cost(
            WEIGHT_HINT, 4 * rows * hidden_local * (taps * half + rank), 8 * taps * half * hidden_local
        ),
        name="weight_grads",
    )(
        idx,
        *([tokens] * local_taps),
        *[p[0] for p in pieces],
        *([far_tokens] * local_taps),
        *[p[0] for p in far_pieces],
        pack,
        *grads,
        latent[0],
        far_latent[0],
    )


def stack_body(first_ref, second_ref, out_ref):
    out_ref[:, :1] = first_ref[...]
    out_ref[:, 1:] = second_ref[...]


def stacked(first, second):
    return pl.pallas_call(
        stack_body,
        out_shape=jax.ShapeDtypeStruct((first.shape[0], 2) + first.shape[2:], bf16),
        cost_estimate=cost(STACK_HINT, first.size, 4 * first.size),
        name="stacked",
    )(first, second)


def inputs_body(n_terms, idx_ref, *refs):
    take = taken(refs)
    total = rows_of(take(2))
    for _ in range(n_terms):
        total = total + rows_of(take(2)).astype(f32)
    left_ref, latent_ref, far_latent_ref, tokens_ref, far_tokens_ref = take(5)
    input_ref, left_grad_ref = take(2)
    order = [k ^ idx_ref[0] for k in range(latent_ref.shape[0])]
    latent = jnp.concatenate([latent_ref[k] for k in order], axis=0)
    far_latent = jnp.concatenate([far_latent_ref[k] for k in order], axis=0)
    low_rank = lax.dot_general(latent, left_ref[...], NT, preferred_element_type=f32)
    input_ref[...] = (total + low_rank).astype(bf16)
    tokens = in_dp_order(idx_ref, tokens_ref[...], far_tokens_ref[...])
    latents = in_dp_order(idx_ref, latent, far_latent)
    left = lax.dot_general(tokens, latents, TN, preferred_element_type=f32)
    left_grad_ref[...] = left.astype(bf16)


def latent_spec(pair):
    return pl.BlockSpec(
        (pair[0].shape[0], None) + pair[0].shape[2:], lambda g, idx: (0, pair[1], 0, 0)
    )


def input_grads(idx, local, terms, left, latent, far_latent, tokens, far_tokens, block):
    block = 2 * block
    width, rank = left.shape
    chunk_rows = local[0].shape[0]
    rows = 2 * chunk_rows
    chunk_spec = pl.BlockSpec((chunk_rows, block), lambda g, idx: (0, g))
    token_spec = pl.BlockSpec((rows, block), lambda g, idx: (0, g))
    left_spec = pl.BlockSpec((block, rank), lambda g, idx: (g, 0))
    return pl.pallas_call(
        functools.partial(inputs_body, len(terms)),
        grid_spec=pltpu.PrefetchScalarGridSpec(
            num_scalar_prefetch=1,
            grid=(width // block,),
            in_specs=[chunk_spec] * (2 + 2 * len(terms))
            + [left_spec, latent_spec(latent), latent_spec(far_latent)]
            + [token_spec, token_spec],
            out_specs=[token_spec, left_spec],
        ),
        out_shape=[
            jax.ShapeDtypeStruct((rows, width), bf16),
            jax.ShapeDtypeStruct((width, rank), bf16),
        ],
        compiler_params=params(),
        cost_estimate=cost(INPUT_HINT, 6 * rows * width * rank, 20 * rows * width),
        name="input_grads",
    )(
        idx,
        *local,
        *[c for pair in terms for c in pair],
        left,
        latent[0],
        far_latent[0],
        tokens,
        far_tokens,
    )


def after(value, *first):
    return lax.optimization_barrier((value, first))[0]


def one_step(f, *args):
    shapes = jax.eval_shape(f, *args)
    other = lambda *_: jax.tree.map(lambda x: jnp.zeros(x.shape, x.dtype), shapes)
    return lax.cond(lax.axis_index("mp") >= 0, f, other, *args)


def halved_sum(halves, bit):
    mine = (lax.axis_index("mp") >> bit) & 1
    sent = jnp.where(mine == 0, halves[1], halves[0])
    kept = jnp.where(mine == 0, halves[0], halves[1])
    return kept + from_partner(sent, "mp", bit)


def high_sum(part, first_bit=2):
    for bit in range(first_bit, lax.axis_size("mp").bit_length() - 1):
        part = part + from_partner(part, "mp", bit)
    return part.astype(bf16)[None, None]


def gathered(stack):
    for bit in (1, 0):
        stack = jnp.concatenate([stack, from_partner(stack, "mp", bit)], axis=0)
    return stack


def with_places(arrays, places):
    return [[(a, *p) for a, p in zip(*tap)] for tap in zip(arrays, places)]


def over_high_terms(terms, *first):
    return [from_partner(after(t, *first), "mp", bit) for bit, t in enumerate(terms) if bit >= 2]


def on_device(tokens, block_weight, left_factor, right_factor, out_cotangent):
    rows, width = tokens.shape
    taps, block, _ = block_weight.shape
    groups = width // block
    local_bits = groups.bit_length() - 1
    high_bits = range(2, taps - 1 - local_bits)
    mp_index = lax.axis_index("mp")
    dp_index = lax.axis_index("dp")
    place = 2 * (mp_index & 1) + ((mp_index >> 1) & 1)
    idx = jnp.stack([place, dp_index]).astype(jnp.int32)
    mine = dp_index.reshape(1).astype(jnp.int32)
    theirs = 1 - mine
    half_rows = rows // 2

    over_high = lambda x: [from_partner(x, "mp", bit) for bit in high_bits]
    cut = half_rows // 2
    first = over_high(tokens[:cut])

    def low_part(tokens, left):
        part = jnp.dot(tokens, left, preferred_element_type=f32)
        part = halved_sum(jnp.split(part, 2, axis=0), 0)
        core = from_partner(after(tokens, part), "mp", 0)
        tokens = after(tokens, part)
        slices = [tokens[:half_rows], tokens[cut:half_rows], tokens[half_rows:]]
        return halved_sum(jnp.split(part, 2, axis=0), 1), core, slices

    def high_part(part, tokens, y_rows, rest, first):
        far_tokens = from_partner(tokens, "dp", 0)
        near_y = from_partner(y_rows, "mp", 1)
        stack = high_sum(part)
        second = over_high(after(rest, stack))
        far = from_partner(stack, "dp", 0)
        stack = jnp.concatenate([stack, from_partner(after(stack, near_y), "mp", 1)], axis=0)
        far_half = column_halves(mine, [far_tokens], block)
        stack = jnp.concatenate([stack, from_partner(after(stack, far, far_half), "mp", 0)], axis=0)
        high = [p for pair in zip(first, second) for p in pair]
        return stack, far, far_tokens, far_half, near_y, second, column_halves(theirs, high, block)

    low_sum, core, slices = one_step(low_part, tokens, left_factor)
    low_sum, first = after((low_sum, first))
    latent, far_quarter, far_tokens, far_half, near_y, second, halves = one_step(
        high_part, low_sum, tokens, *slices[:2], first
    )
    rest = after(slices[2], latent)
    third = over_high(rest)
    far_y = from_partner(rest, "mp", 1)
    received = [
        [[(core, 0, half_rows)], [(near_y, 0, half_rows)]]
        + [[(p, 0, cut), (q, 0, half_rows - cut)] for p, q in zip(first, second)],
        [[(core, 1, half_rows)], [(far_y, 0, half_rows)]] + [[(p, 0, half_rows)] for p in third],
    ]

    far_halves = from_partner(halves, "dp", 0)
    forward = functools.partial(forward_chunk, idx=idx, tokens=tokens, latent=latent)
    forward = functools.partial(forward, weight=block_weight, right=right_factor, cotangent=out_cotangent)
    act, near_grad, near_out, near_local, near_latent = forward(
        0, remote=received[0], act_before=None, packed=0
    )
    far_near_grad = from_partner(after(near_grad, far_halves), "dp", 0)
    near_terms = over_high_terms(near_out, far_y)
    far_y_half = from_partner(after(far_half, near_grad, third), "mp", 1)
    act, grad, far_out, far_local, far_latent_term = forward(
        1, remote=received[1], act_before=act, packed=len(high_bits)
    )
    far_far_grad = from_partner(grad, "dp", 0)
    local = [near_local, far_local]
    grads = [near_grad, grad, far_near_grad, far_far_grad]

    def low_grad(a, b):
        return halved_sum(jnp.split(halved_sum([a, b], 0), 2, axis=0), 1)

    def high_grad(part, *terms):
        return high_sum(part), [from_partner(t, "mp", bit) for bit, t in enumerate(terms)]

    def gather_grad(stack, core_term, far_half):
        stack = jnp.concatenate([stack, from_partner(stack, "mp", 1)], axis=0)
        core_term = from_partner(core_term, "mp", 0)
        stack, core_term = after((stack, core_term))
        far_core = from_partner(after(far_half, stack), "mp", 0)
        return jnp.concatenate([stack, from_partner(stack, "mp", 0)], axis=0), core_term, far_core

    near_latent, far_near_grad = after((near_latent, far_near_grad))
    low_sum = one_step(low_grad, near_latent, far_latent_term)
    low_sum, far_y_half, near_terms = after((low_sum, far_y_half, near_terms))
    quarter_sum, low_terms = one_step(high_grad, low_sum, *near_out[:2])
    far_terms = over_high_terms(far_out, quarter_sum)
    near_terms = low_terms + near_terms
    gathered_both, core_term, far_core = one_step(
        gather_grad, stacked(quarter_sum, far_quarter), far_out[0], far_half
    )

    def last_part(gathered_both, y_term, tokens, remote, far_tokens, far_remote, grads, latent):
        far_latent_grad = from_partner(gathered_both[:, :1], "dp", 0)
        y_term = from_partner(y_term, "mp", 1)
        weights = weight_grads(
            idx,
            tokens,
            with_places(remote, near_places),
            far_tokens,
            with_places(far_remote, far_places),
            grads,
            (latent, 0),
            (gathered_both, 1),
            taps,
            block,
        )
        return far_latent_grad, y_term, *weights

    remote = [a + b for a, b in zip(*received)]
    far_remote = [[(c, 0, rows)] for c in (far_core, far_y_half)]
    far_remote += [[(far_halves, k, half_rows)] for k in range(len(high_bits))]
    near_places, far_places = [[[p[1:] for p in tap] for tap in r] for r in (remote, far_remote)]
    remote, far_remote = [[[p[0] for p in tap] for tap in r] for r in (remote, far_remote)]
    far_latent_grad, y_term, weight_grad, right_grad = one_step(
        last_part, gathered_both, far_out[1], tokens, remote, far_tokens, far_remote, grads, latent
    )
    far_terms = [core_term, y_term] + far_terms
    input_grad, left_grad = input_grads(
        idx,
        local,
        list(zip(near_terms, far_terms)),
        left_factor,
        (gathered_both, 0),
        (far_latent_grad, 0),
        tokens,
        far_tokens,
        block,
    )
    return act, input_grad, weight_grad, left_grad, right_grad


def flip_groups(blocks, distance):
    full_shape = blocks.shape
    group_count = full_shape[1]
    split_view = blocks.reshape(
        (full_shape[0], group_count // (2 * distance), 2, distance) + full_shape[2:]
    )
    return jnp.flip(split_view, axis=2).reshape(full_shape)


def on_device_general(tokens, block_weight, left_factor, right_factor, out_cotangent):
    tok_rows = tokens.shape[0]
    local_width = tokens.shape[1]
    tap_count = block_weight.shape[0]
    block_size = block_weight.shape[1]
    hidden_local = block_weight.shape[2]
    group_count = local_width // block_size
    local_bits = group_count.bit_length() - 1
    tok_blocks = tokens.reshape(tok_rows, group_count, block_size)
    tap_inputs = [tok_blocks]
    for tap_index in range(1, tap_count):
        level_bit = tap_index - 1
        if level_bit < local_bits:
            tap_inputs.append(flip_groups(tok_blocks, 1 << level_bit))
        else:
            partner = from_partner(tokens, "mp", level_bit - local_bits)
            tap_inputs.append(partner.reshape(tok_rows, group_count, block_size))
    stacked = jnp.stack(tap_inputs, axis=2)
    weight_view = block_weight.reshape(tap_count, block_size, group_count, 2 * block_size)
    butterfly = jnp.einsum("tgkc,kcgh->tgh", stacked, weight_view, preferred_element_type=f32)
    butterfly = butterfly.reshape(tok_rows, hidden_local)
    latent = lax.psum(jnp.dot(tokens, left_factor, preferred_element_type=f32), "mp")
    latent_bf = latent.astype(bf16)
    preact = butterfly + jnp.dot(latent_bf, right_factor, preferred_element_type=f32)
    value, slope = gelu_parts(preact)
    activated = value.astype(bf16)
    grad_pre = (out_cotangent.astype(f32) * slope).astype(bf16)
    latent_term = lax.dot_general(grad_pre, right_factor, NT, preferred_element_type=f32)
    latent_grad = lax.psum(latent_term, "mp").astype(bf16)
    left_part = lax.dot_general(tokens, latent_grad, TN, preferred_element_type=f32)
    right_part = lax.dot_general(latent_bf, grad_pre, TN, preferred_element_type=f32)
    left_sum, right_sum = lax.psum((left_part, right_part), "dp")
    grad_view = grad_pre.reshape(tok_rows, group_count, 2 * block_size)
    spread = jnp.einsum("tgh,kcgh->tgkc", grad_view, weight_view, preferred_element_type=f32)
    input_sum = spread[:, :, 0]
    for tap_index in range(1, tap_count):
        level_bit = tap_index - 1
        piece = spread[:, :, tap_index]
        if level_bit < local_bits:
            input_sum = input_sum + flip_groups(piece, 1 << level_bit)
        else:
            returned = from_partner(
                piece.reshape(tok_rows, local_width), "mp", level_bit - local_bits
            )
            input_sum = input_sum + returned.reshape(tok_rows, group_count, block_size)
    low_rank = lax.dot_general(latent_grad, left_factor, NT, preferred_element_type=f32)
    input_grad = (input_sum.reshape(tok_rows, local_width) + low_rank).astype(bf16)
    partial_value = jnp.einsum("tgkc,tgh->kcgh", stacked, grad_view, preferred_element_type=f32)
    partial_value = partial_value.reshape(tap_count, block_size, hidden_local)
    weight_grad = lax.psum_scatter(partial_value, "dp", scatter_dimension=1, tiled=True).astype(bf16)
    return (activated, input_grad, weight_grad, left_sum.astype(bf16), right_sum.astype(bf16))


def solution(mesh):
    pairs = mesh.shape["dp"] == 2 and mesh.shape["mp"] >= 4
    return jax.shard_map(
        on_device if pairs else on_device_general,
        mesh=mesh,
        in_specs=(P("dp", "mp"), P(None, None, "mp"), P("mp", None), P(None, "mp"), P("dp", "mp")),
        out_specs=(P("dp", "mp"), P("dp", "mp"), P(None, "dp", "mp"), P("mp", None), P(None, "mp")),
        check_vma=False,
    )
```
